32 devices in a mesh: stream: 16 (over z, y, core), span: 2 (over x).
Axes of the slice: x: 2, y: 2, z: 4, core: 2. Of those that a mesh axis runs over, the one named last changes fastest.
Arguments:
- basis: float32 [4, 10, 128, 8, 256], P(None, None, 'stream', None, 'span'), may hold values from -6 to 6
- coeffs: float32 [4], replicated, may hold values from -3 to 3
- mixing_matrix: float32 [10, 10], replicated, may hold values from -2 to 2
- base_speed: float32 [128, 8, 256], P('stream', None, 'span'), may hold values from 0.5 to 1.5
- span_speed: float32 [128, 8, 256], P('stream', None, 'span'), may hold values from -2.4 to 2.4
- polymer_gain: float32 [128, 8, 256], P('stream', None, 'span'), may hold values from 0.3 to 3
Outputs:
- proj: float32 [4, 4], replicated
- rfactor: float32 [4, 4], replicated
- basis_new: float32 [4, 10, 128, 8, 256], P(None, None, 'stream', None, 'span')
The draws below stay inside these ranges and needn't reach their ends.
All inputs are finite; a program needn't handle non-finite values.
Results may differ from the reference program's by a relative error of at most 0.00025.
Values sent between devices are 32-bit elements; how exact they have to be, the bound alone decides.
A program may use at most 64 MiB of HBM per device.

```python
import math
import jax
import jax.numpy as jnp
from jax import lax

F = 10
NY = 8
M = 4
STEPS = 4
NX = 128
NZ = 256
NTOT = 2621440


def shard_levels(own_key, shape, split, least, high):
    gain = 1.0
    for dim, parts in split:
        steps = jax.random.uniform(jax.random.fold_in(jax.random.fold_in(own_key, 6), dim), (parts,), jnp.float32, least / len(split), high / len(split))
        gain = gain * jnp.repeat(jnp.exp(steps), shape[dim] // parts).reshape((-1,) + (1,) * (len(shape) - 1 - dim))
    return gain


def noise(key, dims, width, bound, pieces=(), held_as=jnp.bfloat16):
    values = jax.random.normal(key, dims, jnp.float32) * width
    if len(pieces) > 0:
        values = shard_levels(key, dims, pieces, -0.22, 0.18) * values
    return jnp.clip(values, min=-bound, max=bound).astype(held_as)


def setup_inputs(seed: int = 0) -> dict:
    key_list = jax.random.split(jax.random.key(seed), 7)
    basis = noise(key_list[0], (M, F, NX, NY, NZ), 1.0, 6.0, ((2, 16), (4, 2)), jnp.float32)
    coeffs = noise(key_list[1], (M,), 0.5, 3.0, (), jnp.float32)
    mixing_matrix = noise(key_list[2], (F, F), F ** -0.5, 2.0, (), jnp.float32)
    base_speed = jnp.clip(0.5 + 1.0 * jax.random.uniform(key_list[3], (NX, NY, NZ), jnp.float32) ** shard_levels(key_list[3], (NX, NY, NZ), ((0, 16), (2, 2)), -0.2, 0.2), 0.5, 1.5)
    span_speed = noise(key_list[4], (NX, NY, NZ), 0.4, 2.4, ((0, 16), (2, 2)), jnp.float32)
    polymer_gain = jnp.clip(jnp.exp(math.log(3.0) - 2.3025851 * jax.random.uniform(key_list[5], (NX, NY, NZ), jnp.float32) ** shard_levels(key_list[5], (NX, NY, NZ), ((0, 16), (2, 2)), -0.2, 0.2)), 0.3, 3.0)
    return {"basis": basis, "coeffs": coeffs, "mixing_matrix": mixing_matrix, "base_speed": base_speed, "span_speed": span_speed, "polymer_gain": polymer_gain}


def advance(values_now, base_speed, span_speed, polymer_gain, mixing_matrix):
    center_part = values_now[:, 1:-1, :, 1:-1]
    forward_x = values_now[:, 2:, :, 1:-1]
    backward_x = values_now[:, :-2, :, 1:-1]
    forward_z = values_now[:, 1:-1, :, 2:]
    backward_z = values_now[:, 1:-1, :, :-2]
    zero_row = jnp.zeros_like(center_part[:, :, :1, :])
    wall_up = jnp.concatenate([center_part[:, :, 1:, :], zero_row], axis=2)
    wall_down = jnp.concatenate([zero_row, center_part[:, :, :-1, :]], axis=2)
    laplace = forward_x + backward_x + forward_z + backward_z + wall_up + wall_down - 6.0 * center_part
    mixing = jnp.einsum('fg,gxyz->fxyz', mixing_matrix, center_part, precision=lax.Precision.HIGHEST)
    return -base_speed * (forward_x - backward_x) * 0.5 - span_speed * (forward_z - backward_z) * 0.5 + 0.05 * laplace + polymer_gain * mixing

def reference(basis, coeffs, mixing_matrix, base_speed, span_speed, polymer_gain):
    start = jnp.einsum('m,mfxyz->fxyz', coeffs, basis, precision=lax.Precision.HIGHEST)
    current = start
    krylov = []
    for section in range(STEPS):
        padded = jnp.pad(current, ((0, 0), (1, 1), (0, 0), (1, 1)), mode='wrap')
        current = advance(padded, base_speed, span_speed, polymer_gain, mixing_matrix)
        krylov.append(current)
    stacked = jnp.stack(krylov, 0)
    total = float(NTOT)
    flat_basis = basis.reshape(M, -1)
    flat_new = stacked.reshape(STEPS, -1)
    proj = jnp.dot(flat_basis, flat_new.T, precision=lax.Precision.HIGHEST) / total
    projected = flat_new - jnp.dot(proj.T, flat_basis, precision=lax.Precision.HIGHEST)
    gram = jnp.dot(projected, projected.T, precision=lax.Precision.HIGHEST) / total
    lower_factor = jnp.linalg.cholesky(gram)
    solved = jax.scipy.linalg.solve_triangular(lower_factor, projected, lower=True)
    return (proj, lower_factor.T, solved.reshape(stacked.shape))
```

```python
import functools

import jax
import jax.numpy as jnp
from jax import lax
from jax.experimental import pallas as pl
from jax.experimental.pallas import tpu as pltpu
from jax.sharding import PartitionSpec as P

STEPS = 4
DEEP = 4
WIDE = 2 * DEEP
MESH = pl.DeviceIdType.MESH


def total(terms):
    terms = list(terms)
    while len(terms) > 1:
        pairs = [terms[i] + terms[i + 1] for i in range(0, len(terms) - 1, 2)]
        terms = pairs + terms[len(terms) - len(terms) % 2 :]
    return terms[0]


def span_offsets(span):
    return () if span == 1 else ((1,) if span == 2 else (-1, 1))


def partners(span):
    dzs = span_offsets(span)
    return [(dx, 0) for dx in (-1, 1)] + [(0, dz) for dz in dzs] + [
        (dx, dz) for dx in (-1, 1) for dz in dzs
    ]


def krylov_kernel(
    streams, spans,
    coeffs, mix, basis, base, span_speed, gain,
    krylov_out, sums_out,
    ext, state, held, pack, packs, strips, coef, strip_coef, acc, rows, gathered,
    in_sem, out_sem, send_sem, recv_sem, row_send, row_recv,
):
    m, fields, planes = basis.shape[0], basis.shape[1], basis.shape[2]
    steps = STEPS
    lanes = basis.shape[4]
    n = streams * spans
    all_fields = fields + 3
    sx, sz = lax.axis_index("stream"), lax.axis_index("span")
    me = sx * spans + sz

    def device(dx, dz):
        return (lax.rem(sx + dx + streams, streams), lax.rem(sz + dz + spans, spans))

    barrier = pltpu.get_barrier_semaphore()

    def greet(d, carry):
        other = lax.rem(me + d, n)
        pl.semaphore_signal(
            barrier, inc=1, device_id=(other // spans, lax.rem(other, spans)), device_id_type=MESH
        )
        return carry

    own = pl.ds(DEEP, planes)
    loads = [
        pltpu.make_async_copy(basis.at[j], held.at[j], in_sem.at[j]) for j in range(m)
    ] + [
        pltpu.make_async_copy(ref, ext.at[fields + i, own], in_sem.at[m + i])
        for i, ref in enumerate((base, span_speed, gain))
    ]
    for load in loads:
        load.start()
    lax.fori_loop(1, n, greet, 0)

    lane = lax.broadcasted_iota(jnp.int32, (8, lanes), 1)
    row = lax.broadcasted_iota(jnp.int32, (8, lanes), 0)

    def packed(field):
        out = jnp.zeros((8, lanes), jnp.float32)
        for x in range(planes):
            at = WIDE * (x + DEEP)
            moved = pltpu.roll(ext[field, DEEP + x], DEEP + at, 1)
            out = jnp.where((lane >= at) & (lane < at + WIDE), moved, out)
        pack[field] = out

    for load in loads:
        load.wait()

    def start_field(f, carry):
        for x in range(planes):
            ext[f, DEEP + x] = total(coeffs[j] * held[j, f, x] for j in range(m))
        packed(f)
        return carry

    lax.fori_loop(0, fields, start_field, 0)
    for i in range(3):
        packed(fields + i)

    pl.semaphore_wait(barrier, n - 1)

    sends = []

    def send(src, dst, dx, dz):
        i = len(sends)
        copy = pltpu.make_async_remote_copy(
            src_ref=src, dst_ref=dst, send_sem=send_sem.at[i], recv_sem=recv_sem.at[i],
            device_id=device(dx, dz), device_id_type=MESH,
        )
        copy.start()
        sends.append(copy)

    send(ext.at[:, pl.ds(planes, DEEP)], ext.at[:, pl.ds(0, DEEP)], 1, 0)
    send(ext.at[:, pl.ds(DEEP, DEEP)], ext.at[:, pl.ds(planes + DEEP, DEEP)], -1, 0)
    slots = partners(spans)
    for i, (dx, dz) in enumerate(slots):
        send(pack, packs.at[i], -dx, -dz)

    upper = [(i, j) for i in range(m) for j in range(i, m)]
    krylov_pairs = [(k, l) for k in range(steps) for l in range(k, steps)]
    zero = jnp.zeros((8, lanes), jnp.float32)

    def basis_products(f, sums):
        for x in range(planes):
            b = [held[j, f, x] for j in range(m)]
            sums = [s + b[i] * b[j] for s, (i, j) in zip(sums, upper)]
        return sums

    basis_sums = lax.fori_loop(0, fields, basis_products, [zero] * len(upper))
    first = m * steps + len(krylov_pairs)
    for i, s in enumerate(basis_sums):
        acc[first + i] = s

    for copy in sends:
        copy.wait_recv()

    def cooked(u, w):
        return (
            0.05 - 0.5 * u, 0.05 + 0.5 * u, 0.05 - 0.5 * w, 0.05 + 0.5 * w
        )

    for x in range(1, planes + 2 * DEEP - 1):
        for i, value in enumerate(cooked(ext[fields, x], ext[fields + 1, x])):
            coef[i, x] = value

    half = DEEP * WIDE
    inside = (lane >= half) & (lane < half + planes * WIDE)
    left_part = lane % WIDE < DEEP

    def strip_pair(f):
        def whole(dz):
            here = pack[f] if dz == 0 else packs[slots.index((0, dz)), f]
            before = packs[slots.index((-1, dz)), f]
            after = packs[slots.index((1, dz)), f]
            beside = jnp.where(lane < lanes // 2, after, before)
            return jnp.where(inside, here, pltpu.roll(beside, lanes // 2, 1))

        mine = whole(0)
        dzs = span_offsets(spans)
        left = whole(dzs[0]) if dzs else mine
        right = left if len(dzs) < 2 else whole(dzs[1])
        return jnp.where(left_part, left, mine), jnp.where(left_part, mine, right)

    def build_strips(f, carry):
        for s, value in enumerate(strip_pair(f)):
            strips[0, f, s] = value
        return carry

    lax.fori_loop(0, fields, build_strips, 0)
    us, ws, gs = (strip_pair(fields + i) for i in range(3))
    for s in range(2):
        for i, value in enumerate(cooked(us[s], ws[s]) + (gs[s],)):
            strip_coef[i, s] = value

    def walls(v):
        up = jnp.where(row < 7, pltpu.roll(v, 7, 0), 0.0)
        down = jnp.where(row > 0, pltpu.roll(v, 1, 0), 0.0)
        return up + down

    def read(k, f, x):
        return ext[f, x] if k == 0 else state[k - 1, f, x]

    writes = []
    for k in range(steps):
        lo, hi = 1 + k, planes + 2 * DEEP - 1 - k

        def field_pair(h, carry, k=k, lo=lo, hi=hi):
            pair = [2 * h, 2 * h + 1]
            weights = [[mix[f, g] for g in range(fields)] for f in pair]
            edges = [
                jnp.where(lane % WIDE == DEEP - 1, strips[k, f, 0],
                          pltpu.roll(strips[k, f, 1], lanes - 2, 1))
                for f in pair
            ]
            for x in range(lo, hi):
                vs = [read(k, g, x) for g in range(fields)]
                for f, weight, edge in zip(pair, weights, edges):
                    mixed = total(a * v for a, v in zip(weight, vs))
                    v = read(k, f, x)
                    rim = pltpu.roll(edge, (2 * lanes - (WIDE * x + DEEP - 1)) % lanes, 1)
                    ahead = jnp.where(lane == lanes - 1, rim, pltpu.roll(v, lanes - 1, 1))
                    behind = jnp.where(lane == 0, rim, pltpu.roll(v, 1, 1))
                    state[k, f, x] = (
                        (coef[0, x] * read(k, f, x + 1) + coef[1, x] * read(k, f, x - 1))
                        + (coef[2, x] * ahead + coef[3, x] * behind)
                        + (0.05 * walls(v) - 0.3 * v)
                        + ext[fields + 2, x] * mixed
                    )
            if k < steps - 1:
                for s in range(2):
                    vs = [strips[k, g, s] for g in range(fields)]
                    for f, weight in zip(pair, weights):
                        mixed = total(a * v for a, v in zip(weight, vs))
                        v = strips[k, f, s]
                        strips[k + 1, f, s] = (
                            strip_coef[0, s] * pltpu.roll(v, lanes - WIDE, 1)
                            + strip_coef[1, s] * pltpu.roll(v, WIDE, 1)
                            + strip_coef[2, s] * pltpu.roll(v, lanes - 1, 1)
                            + strip_coef[3, s] * pltpu.roll(v, 1, 1)
                            + (0.05 * walls(v) - 0.3 * v)
                            + strip_coef[4, s] * mixed
                        )
            return carry

        lax.fori_loop(0, fields // 2, field_pair, 0)
        write = pltpu.make_async_copy(state.at[k, :, own], krylov_out.at[k], out_sem.at[k])
        write.start()
        writes.append(write)

    def new_products(f, sums):
        for x in range(planes):
            b = [held[j, f, x] for j in range(m)]
            v = [state[k, f, DEEP + x] for k in range(steps)]
            terms = [b[j] * v[k] for j in range(m) for k in range(steps)]
            terms += [v[k] * v[l] for k, l in krylov_pairs]
            sums = [s + t for s, t in zip(sums, terms)]
        return sums

    new_sums = lax.fori_loop(0, fields, new_products, [zero] * first)
    count = first + len(upper)
    for i, s in enumerate(new_sums):
        rows[pl.ds(i, 1)] = jnp.sum(s, axis=0, keepdims=True)
    for i in range(first, count):
        rows[pl.ds(i, 1)] = jnp.sum(acc[i], axis=0, keepdims=True)
    for i in range(count, rows.shape[0]):
        rows[pl.ds(i, 1)] = jnp.zeros((1, lanes), jnp.float32)
    sums = jnp.sum(rows[...], axis=1, keepdims=True)
    at = lax.broadcasted_iota(jnp.int32, rows.shape, 0)
    spot = lax.broadcasted_iota(jnp.int32, rows.shape, 1)
    gathered[me] = jnp.sum(jnp.where(at == spot, sums, 0.0), axis=0, keepdims=True)

    def row_copy(d):
        other = lax.rem(me + d, n)
        return pltpu.make_async_remote_copy(
            src_ref=gathered.at[me], dst_ref=gathered.at[me], send_sem=row_send, recv_sem=row_recv,
            device_id=(other // spans, lax.rem(other, spans)), device_id_type=MESH,
        )

    def share(d, carry):
        row_copy(d).start()
        return carry

    lax.fori_loop(1, n, share, 0)
    others = gathered.at[pl.ds(0, n - 1)]
    everyone = pltpu.make_async_remote_copy(
        src_ref=others, dst_ref=others, send_sem=row_send, recv_sem=row_recv,
        device_id=device(1, 0), device_id_type=MESH,
    )
    everyone.wait_recv()
    sums_out[...] = jnp.sum(gathered[...], axis=0)
    everyone.wait_send()
    for copy in sends:
        copy.wait_send()
    for write in writes:
        write.wait()


def finish_kernel(
    ntot, chunks,
    sums, basis, krylov,
    proj_out, rfactor_out, new_out,
    held, vectors, result, basis_sem, krylov_sem, out_sem,
):
    m, fields, planes = basis.shape[0], basis.shape[1], basis.shape[2]
    steps = krylov.shape[0]
    part = fields // chunks

    def piece(c):
        return pl.ds(c * part, part)

    loads = []
    for c in range(chunks):
        loads.append((
            pltpu.make_async_copy(basis.at[:, piece(c)], held.at[:, piece(c)], basis_sem.at[c]),
            pltpu.make_async_copy(krylov.at[:, piece(c)], vectors.at[:, piece(c)], krylov_sem.at[c]),
        ))
        for load in loads[-1]:
            load.start()

    shape = (8, basis.shape[4])
    row = sums[...] * (1.0 / ntot)

    def value(i):
        return jnp.broadcast_to(row[:, i : i + 1], shape)

    p = [[value(steps * j + k) for k in range(steps)] for j in range(m)]
    at = m * steps
    kk, bb = {}, {}
    for k in range(steps):
        for l in range(k, steps):
            kk[k, l] = value(at)
            at += 1
    for i in range(m):
        for j in range(i, m):
            bb[i, j] = bb[j, i] = value(at)
            at += 1
    q = [
        [2.0 * p[i][l] - total(bb[i, j] * p[j][l] for j in range(m)) for l in range(steps)]
        for i in range(m)
    ]
    low, inverse = {}, []
    for l in range(steps):
        for k in range(l, steps):
            g = kk[l, k] - total(p[i][l] * q[i][k] for i in range(m))
            for j in range(l):
                g = g - low[k, j] * low[l, j]
            if k == l:
                low[l, l] = jnp.sqrt(g)
                inverse.append(1.0 / low[l, l])
            else:
                low[k, l] = g * inverse[l]

    x = lax.broadcasted_iota(jnp.int32, shape, 0)
    y = lax.broadcasted_iota(jnp.int32, shape, 1)
    proj = jnp.zeros(shape, jnp.float32)
    for j in range(m):
        for k in range(steps):
            proj = jnp.where((x == j) & (y == k), p[j][k], proj)
    proj_out[...] = proj[:m, :steps]
    factor = jnp.zeros(shape, jnp.float32)
    for k, l in low:
        factor = jnp.where((x == l) & (y == k), low[k, l], factor)
    rfactor_out[...] = factor[:steps, :steps]

    writes = []
    for c in range(chunks):
        for load in loads[c]:
            load.wait()

        def one(i, carry, c=c):
            f = c * part + i
            for s in range(planes):
                b = [held[j, f, s] for j in range(m)]
                done = []
                for k in range(steps):
                    v = vectors[k, f, s] - total(p[j][k] * b[j] for j in range(m))
                    for l in range(k):
                        v = v - low[k, l] * done[l]
                    done.append(v * inverse[k])
                    result[k, f, s] = done[k]
            return carry

        lax.fori_loop(0, part, one, 0)
        write = pltpu.make_async_copy(
            result.at[:, piece(c)], new_out.at[:, piece(c)], out_sem.at[c]
        )
        write.start()
        writes.append(write)
    for write in writes:
        write.wait()


def on_device(streams, spans, basis, coeffs, mixing_matrix, base_speed, span_speed, polymer_gain):
    m, fields, planes, height, lanes = basis.shape
    n = streams * spans
    f32 = jnp.float32
    deep = planes + 2 * DEEP
    count = m * STEPS + STEPS * (STEPS + 1) // 2 + m * (m + 1) // 2
    padded = -(-count // 8) * 8
    links = 2 + len(partners(spans))
    smem = pl.BlockSpec(memory_space=pltpu.SMEM)
    hbm = pl.BlockSpec(memory_space=pl.ANY)
    vmem = pl.BlockSpec(memory_space=pltpu.VMEM)
    vector = (fields, planes, height, lanes)
    krylov, sums = pl.pallas_call(
        functools.partial(krylov_kernel, streams, spans),
        out_shape=(
            jax.ShapeDtypeStruct((STEPS,) + vector, f32),
            jax.ShapeDtypeStruct((1, lanes), f32),
        ),
        in_specs=[smem, smem, hbm, hbm, hbm, hbm],
        out_specs=(hbm, vmem),
        scratch_shapes=[
            pltpu.VMEM((fields + 3, deep, height, lanes), f32),
            pltpu.VMEM((STEPS, fields, deep, height, lanes), f32),
            pltpu.VMEM((m,) + vector, f32),
            pltpu.VMEM((fields + 3, height, lanes), f32),
            pltpu.VMEM((links - 2, fields + 3, height, lanes), f32),
            pltpu.VMEM((STEPS, fields, 2, height, lanes), f32),
            pltpu.VMEM((4, deep, height, lanes), f32),
            pltpu.VMEM((5, 2, height, lanes), f32),
            pltpu.VMEM((count, height, lanes), f32),
            pltpu.VMEM((padded, lanes), f32),
            pltpu.VMEM((n, 1, lanes), f32),
            pltpu.SemaphoreType.DMA((m + 3,)),
            pltpu.SemaphoreType.DMA((STEPS,)),
            pltpu.SemaphoreType.DMA((links,)),
            pltpu.SemaphoreType.DMA((links,)),
            pltpu.SemaphoreType.DMA,
            pltpu.SemaphoreType.DMA,
        ],
        compiler_params=pltpu.CompilerParams(
            collective_id=0, has_side_effects=True, vmem_limit_bytes=24 * 2**20
        ),
        name="krylov",
    )(coeffs, mixing_matrix, basis, base_speed, span_speed, polymer_gain)
    chunks = 5 if fields % 5 == 0 else 1
    return pl.pallas_call(
        functools.partial(finish_kernel, float(m and basis[0].size * n), chunks),
        out_shape=(
            jax.ShapeDtypeStruct((m, STEPS), f32),
            jax.ShapeDtypeStruct((STEPS, STEPS), f32),
            jax.ShapeDtypeStruct((STEPS,) + vector, f32),
        ),
        in_specs=[vmem, hbm, hbm],
        out_specs=(vmem, vmem, hbm),
        scratch_shapes=[
            pltpu.VMEM((m,) + vector, f32),
            pltpu.VMEM((STEPS,) + vector, f32),
            pltpu.VMEM((STEPS,) + vector, f32),
            pltpu.SemaphoreType.DMA((chunks,)),
            pltpu.SemaphoreType.DMA((chunks,)),
            pltpu.SemaphoreType.DMA((chunks,)),
        ],
        compiler_params=pltpu.CompilerParams(vmem_limit_bytes=24 * 2**20),
        name="finish",
    )(sums, basis, krylov)


def solution(mesh):
    placed = (
        P(None, None, "stream", None, "span"),
        P(),
        P(),
        P("stream", None, "span"),
        P("stream", None, "span"),
        P("stream", None, "span"),
    )
    return jax.shard_map(
        functools.partial(on_device, mesh.shape["stream"], mesh.shape["span"]),
        mesh=mesh,
        in_specs=placed,
        out_specs=(P(), P(), P(None, None, "stream", None, "span")),
        check_vma=False,
    )
```

```python
import functools

import jax
import jax.numpy as jnp
from jax import lax
from jax.experimental import pallas as pl
from jax.experimental.pallas import tpu as pltpu
from jax.sharding import PartitionSpec as P

STEPS = 4
DEEP = 4
WIDE = 2 * DEEP
MESH = pl.DeviceIdType.MESH


def total(terms):
    terms = list(terms)
    while len(terms) > 1:
        pairs = [terms[i] + terms[i + 1] for i in range(0, len(terms) - 1, 2)]
        terms = pairs + terms[len(terms) - len(terms) % 2 :]
    return terms[0]


def span_offsets(span):
    return () if span == 1 else ((1,) if span == 2 else (-1, 1))


def partners(span):
    dzs = span_offsets(span)
    return [(dx, 0) for dx in (-1, 1)] + [(0, dz) for dz in dzs] + [
        (dx, dz) for dx in (-1, 1) for dz in dzs
    ]


def krylov_kernel(
    streams, spans,
    coeffs_in, mix_in, basis, base, span_speed, gain,
    krylov_out, sums_out,
    ext, states, held, pack, packs, strips, coef, strip_coef, acc, rows, gathered, coeffs, mix,
    in_sem, out_sem, send_sem, recv_sem, row_send, row_recv,
):
    m, fields, planes = basis.shape[0], basis.shape[1], basis.shape[2]
    steps = STEPS
    lanes = basis.shape[4]
    n = streams * spans
    all_fields = fields + 3
    sx, sz = lax.axis_index("stream"), lax.axis_index("span")
    me = sx * spans + sz

    def device(dx, dz):
        return (lax.rem(sx + dx + streams, streams), lax.rem(sz + dz + spans, spans))

    barrier = pltpu.get_barrier_semaphore()

    def greet(d, carry):
        other = lax.rem(me + d, n)
        pl.semaphore_signal(
            barrier, inc=1, device_id=(other // spans, lax.rem(other, spans)), device_id_type=MESH
        )
        return carry

    own = pl.ds(DEEP, planes)
    loads = [
        pltpu.make_async_copy(basis.at[j], held.at[j], in_sem.at[j]) for j in range(m)
    ] + [
        pltpu.make_async_copy(ref, ext.at[fields + i, own], in_sem.at[m + i])
        for i, ref in enumerate((base, span_speed, gain))
    ] + [
        pltpu.make_async_copy(coeffs_in, coeffs, in_sem.at[m + 3]),
        pltpu.make_async_copy(mix_in, mix, in_sem.at[m + 4]),
    ]
    for load in loads:
        load.start()
    lax.fori_loop(1, n, greet, 0)

    lane = lax.broadcasted_iota(jnp.int32, (8, lanes), 1)
    row = lax.broadcasted_iota(jnp.int32, (8, lanes), 0)

    def packed(field, values):
        out = jnp.zeros((8, lanes), jnp.float32)
        for x in range(planes):
            at = WIDE * (x + DEEP)
            moved = pltpu.roll(values[x], DEEP + at, 1)
            out = jnp.where((lane >= at) & (lane < at + WIDE), moved, out)
        pack[field] = out

    for load in loads:
        load.wait()

    weights = [coeffs[j] for j in range(m)]

    def start_field(f, carry):
        values = [total(weights[j] * held[j, f, x] for j in range(m)) for x in range(planes)]
        for x in range(planes):
            ext[f, DEEP + x] = values[x]
        packed(f, values)
        return carry

    lax.fori_loop(0, fields, start_field, 0)
    for i in range(3):
        packed(fields + i, [ext[fields + i, DEEP + x] for x in range(planes)])

    pl.semaphore_wait(barrier, n - 1)

    sends = []

    def send(src, dst, dx, dz):
        i = len(sends)
        copy = pltpu.make_async_remote_copy(
            src_ref=src, dst_ref=dst, send_sem=send_sem.at[i], recv_sem=recv_sem.at[i],
            device_id=device(dx, dz), device_id_type=MESH,
        )
        copy.start()
        sends.append(copy)

    send(ext.at[:, pl.ds(planes, DEEP)], ext.at[:, pl.ds(0, DEEP)], 1, 0)
    send(ext.at[:, pl.ds(DEEP, DEEP)], ext.at[:, pl.ds(planes + DEEP, DEEP)], -1, 0)
    slots = partners(spans)
    for i, (dx, dz) in enumerate(slots):
        send(pack, packs.at[i], -dx, -dz)

    upper = [(i, j) for i in range(m) for j in range(i, m)]
    krylov_pairs = [(k, l) for k in range(steps) for l in range(k, steps)]
    zero = jnp.zeros((8, lanes), jnp.float32)

    def basis_products(f, sums):
        for x in range(planes):
            b = [held[j, f, x] for j in range(m)]
            sums = [s + b[i] * b[j] for s, (i, j) in zip(sums, upper)]
        return sums

    basis_sums = lax.fori_loop(0, fields, basis_products, [zero] * len(upper))
    first = m * steps + len(krylov_pairs)
    for i, s in enumerate(basis_sums):
        acc[first + i] = s

    for copy in sends:
        copy.wait_recv()

    def cooked(u, w):
        return (
            0.05 - 0.5 * u, 0.05 + 0.5 * u, 0.05 - 0.5 * w, 0.05 + 0.5 * w
        )

    for x in range(1, planes + 2 * DEEP - 1):
        for i, value in enumerate(cooked(ext[fields, x], ext[fields + 1, x])):
            coef[i, x] = value

    half = DEEP * WIDE
    inside = (lane >= half) & (lane < half + planes * WIDE)
    left_part = lane % WIDE < DEEP

    def strip_pair(f):
        def whole(dz):
            here = pack[f] if dz == 0 else packs[slots.index((0, dz)), f]
            before = packs[slots.index((-1, dz)), f]
            after = packs[slots.index((1, dz)), f]
            beside = jnp.where(lane < lanes // 2, after, before)
            return jnp.where(inside, here, pltpu.roll(beside, lanes // 2, 1))

        mine = whole(0)
        dzs = span_offsets(spans)
        left = whole(dzs[0]) if dzs else mine
        right = left if len(dzs) < 2 else whole(dzs[1])
        return jnp.where(left_part, left, mine), jnp.where(left_part, mine, right)

    def build_strips(f, carry):
        for s, value in enumerate(strip_pair(f)):
            strips[0][f, s] = value
        return carry

    lax.fori_loop(0, fields, build_strips, 0)
    us, ws, gs = (strip_pair(fields + i) for i in range(3))
    for s in range(2):
        for i, value in enumerate(cooked(us[s], ws[s]) + (gs[s],)):
            strip_coef[i, s] = value

    def walls(v):
        up = jnp.where(row < 7, pltpu.roll(v, 7, 0), 0.0)
        down = jnp.where(row > 0, pltpu.roll(v, 1, 0), 0.0)
        return up + down

    def read(k, f, x):
        return ext[f, x] if k == 0 else states[k - 1][f, x]

    writes = []
    for k in range(steps):
        lo, hi = 1 + k, planes + 2 * DEEP - 1 - k

        def field_pair(h, carry, k=k, lo=lo, hi=hi):
            pair = [2 * h, 2 * h + 1]
            weights = [[mix[f, g] for g in range(fields)] for f in pair]
            edges = [
                jnp.where(lane % WIDE == DEEP - 1, strips[k][f, 0],
                          pltpu.roll(strips[k][f, 1], lanes - 2, 1))
                for f in pair
            ]
            for x in range(lo, hi):
                vs = [read(k, g, x) for g in range(fields)]
                for f, weight, edge in zip(pair, weights, edges):
                    mixed = total(a * v for a, v in zip(weight, vs))
                    v = read(k, f, x)
                    rim = pltpu.roll(edge, (2 * lanes - (WIDE * x + DEEP - 1)) % lanes, 1)
                    ahead = jnp.where(lane == lanes - 1, rim, pltpu.roll(v, lanes - 1, 1))
                    behind = jnp.where(lane == 0, rim, pltpu.roll(v, 1, 1))
                    states[k][f, x] = (
                        (coef[0, x] * read(k, f, x + 1) + coef[1, x] * read(k, f, x - 1))
                        + (coef[2, x] * ahead + coef[3, x] * behind)
                        + (0.05 * walls(v) - 0.3 * v)
                        + ext[fields + 2, x] * mixed
                    )
            if k < steps - 1:
                for s in range(2):
                    vs = [strips[k][g, s] for g in range(fields)]
                    for f, weight in zip(pair, weights):
                        mixed = total(a * v for a, v in zip(weight, vs))
                        v = strips[k][f, s]
                        strips[k + 1][f, s] = (
                            strip_coef[0, s] * pltpu.roll(v, lanes - WIDE, 1)
                            + strip_coef[1, s] * pltpu.roll(v, WIDE, 1)
                            + strip_coef[2, s] * pltpu.roll(v, lanes - 1, 1)
                            + strip_coef[3, s] * pltpu.roll(v, 1, 1)
                            + (0.05 * walls(v) - 0.3 * v)
                            + strip_coef[4, s] * mixed
                        )
            return carry

        lax.fori_loop(0, fields // 2, field_pair, 0)
        write = pltpu.make_async_copy(states[k].at[:, own], krylov_out.at[k], out_sem.at[k])
        write.start()
        writes.append(write)

    def new_products(f, sums):
        for x in range(planes):
            b = [held[j, f, x] for j in range(m)]
            v = [states[k][f, DEEP + x] for k in range(steps)]
            terms = [b[j] * v[k] for j in range(m) for k in range(steps)]
            terms += [v[k] * v[l] for k, l in krylov_pairs]
            sums = [s + t for s, t in zip(sums, terms)]
        return sums

    new_sums = lax.fori_loop(0, fields, new_products, [zero] * first)
    count = first + len(upper)
    for i, s in enumerate(new_sums):
        rows[pl.ds(i, 1)] = jnp.sum(s, axis=0, keepdims=True)
    for i in range(first, count):
        rows[pl.ds(i, 1)] = jnp.sum(acc[i], axis=0, keepdims=True)
    for i in range(count, rows.shape[0]):
        rows[pl.ds(i, 1)] = jnp.zeros((1, lanes), jnp.float32)
    sums = jnp.sum(rows[...], axis=1, keepdims=True)
    at = lax.broadcasted_iota(jnp.int32, rows.shape, 0)
    spot = lax.broadcasted_iota(jnp.int32, rows.shape, 1)
    gathered[me] = jnp.sum(jnp.where(at == spot, sums, 0.0), axis=0, keepdims=True)

    def row_copy(d):
        other = lax.rem(me + d, n)
        return pltpu.make_async_remote_copy(
            src_ref=gathered.at[me], dst_ref=gathered.at[me], send_sem=row_send, recv_sem=row_recv,
            device_id=(other // spans, lax.rem(other, spans)), device_id_type=MESH,
        )

    def share(d, carry):
        row_copy(d).start()
        return carry

    lax.fori_loop(1, n, share, 0)
    others = gathered.at[pl.ds(0, n - 1)]
    everyone = pltpu.make_async_remote_copy(
        src_ref=others, dst_ref=others, send_sem=row_send, recv_sem=row_recv,
        device_id=device(1, 0), device_id_type=MESH,
    )
    everyone.wait_recv()
    sums_out[...] = jnp.sum(gathered[...], axis=0)
    everyone.wait_send()
    for copy in sends:
        copy.wait_send()
    for write in writes:
        write.wait()


def finish_kernel(
    ntot, chunks,
    sums, basis, krylov,
    proj_out, rfactor_out, new_out,
    result, out_sem,
):
    m, fields, planes = basis.shape[0], basis.shape[1], basis.shape[2]
    steps = krylov.shape[0]
    part = fields // chunks

    def piece(c):
        return pl.ds(c * part, part)

    shape = (8, basis.shape[4])
    row = sums[...] * (1.0 / ntot)

    def value(i):
        return jnp.broadcast_to(row[:, i : i + 1], shape)

    p = [[value(steps * j + k) for k in range(steps)] for j in range(m)]
    at = m * steps
    kk, bb = {}, {}
    for k in range(steps):
        for l in range(k, steps):
            kk[k, l] = value(at)
            at += 1
    for i in range(m):
        for j in range(i, m):
            bb[i, j] = bb[j, i] = value(at)
            at += 1
    q = [
        [2.0 * p[i][l] - total(bb[i, j] * p[j][l] for j in range(m)) for l in range(steps)]
        for i in range(m)
    ]
    low, inverse = {}, []
    for l in range(steps):
        for k in range(l, steps):
            g = kk[l, k] - total(p[i][l] * q[i][k] for i in range(m))
            for j in range(l):
                g = g - low[k, j] * low[l, j]
            if k == l:
                low[l, l] = jnp.sqrt(g)
                inverse.append(1.0 / low[l, l])
            else:
                low[k, l] = g * inverse[l]

    x = lax.broadcasted_iota(jnp.int32, shape, 0)
    y = lax.broadcasted_iota(jnp.int32, shape, 1)
    proj = jnp.zeros(shape, jnp.float32)
    for j in range(m):
        for k in range(steps):
            proj = jnp.where((x == j) & (y == k), p[j][k], proj)
    proj_out[...] = proj[:m, :steps]
    factor = jnp.zeros(shape, jnp.float32)
    for k, l in low:
        factor = jnp.where((x == l) & (y == k), low[k, l], factor)
    rfactor_out[...] = factor[:steps, :steps]

    writes = []
    for c in range(chunks):
        def one(i, carry, c=c):
            f = c * part + i
            for s in range(planes):
                b = [basis[j, f, s] for j in range(m)]
                done = []
                for k in range(steps):
                    v = krylov[k, f, s] - total(p[j][k] * b[j] for j in range(m))
                    for l in range(k):
                        v = v - low[k, l] * done[l]
                    done.append(v * inverse[k])
                    result[k, f, s] = done[k]
            return carry

        lax.fori_loop(0, part, one, 0)
        write = pltpu.make_async_copy(
            result.at[:, piece(c)], new_out.at[:, piece(c)], out_sem.at[c]
        )
        write.start()
        writes.append(write)
    for write in writes:
        write.wait()


def on_device(streams, spans, basis, coeffs, mixing_matrix, base_speed, span_speed, polymer_gain):
    m, fields, planes, height, lanes = basis.shape
    n = streams * spans
    f32 = jnp.float32
    deep = planes + 2 * DEEP
    count = m * STEPS + STEPS * (STEPS + 1) // 2 + m * (m + 1) // 2
    padded = -(-count // 8) * 8
    links = 2 + len(partners(spans))
    hbm = pl.BlockSpec(memory_space=pltpu.HBM)
    anywhere = pl.BlockSpec(memory_space=pl.ANY)
    vmem = pl.BlockSpec(memory_space=pltpu.VMEM)
    vector = (fields, planes, height, lanes)
    krylov, sums = pl.pallas_call(
        functools.partial(krylov_kernel, streams, spans),
        out_shape=(
            jax.ShapeDtypeStruct((STEPS,) + vector, f32),
            jax.ShapeDtypeStruct((1, lanes), f32),
        ),
        in_specs=[hbm] * 6,
        out_specs=(anywhere, vmem),
        scratch_shapes=[
            pltpu.VMEM((fields + 3, deep, height, lanes), f32),
            [pltpu.VMEM((fields, deep, height, lanes), f32)] * STEPS,
            pltpu.VMEM((m,) + vector, f32),
            pltpu.VMEM((fields + 3, height, lanes), f32),
            pltpu.VMEM((links - 2, fields + 3, height, lanes), f32),
            [pltpu.VMEM((fields, 2, height, lanes), f32)] * STEPS,
            pltpu.VMEM((4, deep, height, lanes), f32),
            pltpu.VMEM((5, 2, height, lanes), f32),
            pltpu.VMEM((count, height, lanes), f32),
            pltpu.VMEM((padded, lanes), f32),
            pltpu.VMEM((n, 1, lanes), f32),
            pltpu.SMEM(coeffs.shape, f32),
            pltpu.SMEM(mixing_matrix.shape, f32),
            pltpu.SemaphoreType.DMA((m + 5,)),
            pltpu.SemaphoreType.DMA((STEPS,)),
            pltpu.SemaphoreType.DMA((links,)),
            pltpu.SemaphoreType.DMA((links,)),
            pltpu.SemaphoreType.DMA,
            pltpu.SemaphoreType.DMA,
        ],
        compiler_params=pltpu.CompilerParams(
            collective_id=0, has_side_effects=True, vmem_limit_bytes=24 * 2**20
        ),
        name="krylov",
    )(*(
        pltpu.with_memory_space_constraint(x, pltpu.HBM)
        for x in (coeffs, mixing_matrix, basis, base_speed, span_speed, polymer_gain)
    ))
    chunks = 5 if fields % 5 == 0 else 1
    return pl.pallas_call(
        functools.partial(finish_kernel, float(m and basis[0].size * n), chunks),
        out_shape=(
            jax.ShapeDtypeStruct((m, STEPS), f32),
            jax.ShapeDtypeStruct((STEPS, STEPS), f32),
            jax.ShapeDtypeStruct((STEPS,) + vector, f32),
        ),
        in_specs=[vmem, vmem, vmem],
        out_specs=(vmem, vmem, hbm),
        scratch_shapes=[
            pltpu.VMEM((STEPS,) + vector, f32),
            pltpu.SemaphoreType.DMA((chunks,)),
        ],
        compiler_params=pltpu.CompilerParams(vmem_limit_bytes=24 * 2**20),
        name="finish",
    )(sums, basis, krylov)


def solution(mesh):
    placed = (
        P(None, None, "stream", None, "span"),
        P(),
        P(),
        P("stream", None, "span"),
        P("stream", None, "span"),
        P("stream", None, "span"),
    )
    return jax.shard_map(
        functools.partial(on_device, mesh.shape["stream"], mesh.shape["span"]),
        mesh=mesh,
        in_specs=placed,
        out_specs=(P(), P(), P(None, None, "stream", None, "span")),
        check_vma=False,
    )
```

```python
import functools

import jax
import jax.numpy as jnp
from jax import lax
from jax.experimental import pallas as pl
from jax.experimental.pallas import tpu as pltpu
from jax.sharding import PartitionSpec as P

STEPS = 4
DEEP = 4
WIDE = 2 * DEEP
MESH = pl.DeviceIdType.MESH


def total(terms):
    terms = list(terms)
    while len(terms) > 1:
        pairs = [terms[i] + terms[i + 1] for i in range(0, len(terms) - 1, 2)]
        terms = pairs + terms[len(terms) - len(terms) % 2 :]
    return terms[0]


def span_offsets(span):
    return () if span == 1 else ((1,) if span == 2 else (-1, 1))


def partners(span):
    dzs = span_offsets(span)
    return [(dx, 0) for dx in (-1, 1)] + [(0, dz) for dz in dzs] + [
        (dx, dz) for dx in (-1, 1) for dz in dzs
    ]


def near_and_far(streams):
    near = 4 if streams % 4 == 0 else 1
    return near, streams // near


def krylov_kernel(
    streams, spans,
    coeffs_in, mix_in, basis, base, span_speed, gain,
    krylov_out, sums_out,
    ext, states, held, pack, packs, strips, coef, strip_coef, acc, rows, near_rows, far_rows, coeffs, mix,
    in_sem, out_sem, send_sem, recv_sem, row_send, row_recv,
):
    m, fields, planes = basis.shape[0], basis.shape[1], basis.shape[2]
    steps = STEPS
    lanes = basis.shape[4]
    sx, sz = lax.axis_index("stream"), lax.axis_index("span")
    near, far = near_and_far(streams)
    near_group = near * spans
    place = lax.rem(sx, near)
    near_index, far_index = place * spans + sz, sx // near

    def near_device(d):
        other = lax.rem(near_index + d, near_group)
        return (sx - place + other // spans, lax.rem(other, spans))

    def far_device(d):
        return (lax.rem(far_index + d, far) * near + place, sz)

    def device(dx, dz):
        return (lax.rem(sx + dx + streams, streams), lax.rem(sz + dz + spans, spans))

    barrier = pltpu.get_barrier_semaphore()

    own = pl.ds(DEEP, planes)
    loads = [
        pltpu.make_async_copy(basis.at[j], held.at[j], in_sem.at[j]) for j in range(m)
    ] + [
        pltpu.make_async_copy(ref, ext.at[fields + i, own], in_sem.at[m + i])
        for i, ref in enumerate((base, span_speed, gain))
    ] + [
        pltpu.make_async_copy(coeffs_in, coeffs, in_sem.at[m + 3]),
        pltpu.make_async_copy(mix_in, mix, in_sem.at[m + 4]),
    ]
    for load in loads:
        load.start()
    slots = partners(spans)
    greeted = [near_device(d) for d in range(1, near_group)]
    greeted += [far_device(d) for d in range(1, far)]
    greeted += [device(dx, dz) for dx, dz in slots]
    for other in greeted:
        pl.semaphore_signal(barrier, inc=1, device_id=other, device_id_type=MESH)

    lane = lax.broadcasted_iota(jnp.int32, (8, lanes), 1)
    row = lax.broadcasted_iota(jnp.int32, (8, lanes), 0)

    def packed(field, values):
        out = jnp.zeros((8, lanes), jnp.float32)
        for x in range(planes):
            at = WIDE * (x + DEEP)
            moved = pltpu.roll(values[x], DEEP + at, 1)
            out = jnp.where((lane >= at) & (lane < at + WIDE), moved, out)
        pack[field] = out

    for load in loads:
        load.wait()

    weights = [coeffs[j] for j in range(m)]

    def start_field(f, carry):
        values = [total(weights[j] * held[j, f, x] for j in range(m)) for x in range(planes)]
        for x in range(planes):
            ext[f, DEEP + x] = values[x]
        packed(f, values)
        return carry

    lax.fori_loop(0, fields, start_field, 0)
    for i in range(3):
        packed(fields + i, [ext[fields + i, DEEP + x] for x in range(planes)])

    pl.semaphore_wait(barrier, len(greeted))

    sends = []

    def send(src, dst, dx, dz):
        i = len(sends)
        copy = pltpu.make_async_remote_copy(
            src_ref=src, dst_ref=dst, send_sem=send_sem.at[i], recv_sem=recv_sem.at[i],
            device_id=device(dx, dz), device_id_type=MESH,
        )
        copy.start()
        sends.append(copy)

    send(ext.at[:, pl.ds(planes, DEEP)], ext.at[:, pl.ds(0, DEEP)], 1, 0)
    send(ext.at[:, pl.ds(DEEP, DEEP)], ext.at[:, pl.ds(planes + DEEP, DEEP)], -1, 0)
    for i, (dx, dz) in enumerate(slots):
        send(pack, packs.at[i], -dx, -dz)

    upper = [(i, j) for i in range(m) for j in range(i, m)]
    krylov_pairs = [(k, l) for k in range(steps) for l in range(k, steps)]
    zero = jnp.zeros((8, lanes), jnp.float32)

    def basis_products(f, sums):
        for x in range(planes):
            b = [held[j, f, x] for j in range(m)]
            sums = [s + b[i] * b[j] for s, (i, j) in zip(sums, upper)]
        return sums

    basis_sums = lax.fori_loop(0, fields, basis_products, [zero] * len(upper))
    first = m * steps + len(krylov_pairs)
    for i, s in enumerate(basis_sums):
        acc[first + i] = s

    for copy in sends:
        copy.wait_recv()

    def cooked(u, w):
        return (
            0.05 - 0.5 * u, 0.05 + 0.5 * u, 0.05 - 0.5 * w, 0.05 + 0.5 * w
        )

    for x in range(1, planes + 2 * DEEP - 1):
        for i, value in enumerate(cooked(ext[fields, x], ext[fields + 1, x])):
            coef[i, x] = value

    half = DEEP * WIDE
    inside = (lane >= half) & (lane < half + planes * WIDE)
    left_part = lane % WIDE < DEEP

    def strip_pair(f):
        def whole(dz):
            here = pack[f] if dz == 0 else packs[slots.index((0, dz)), f]
            before = packs[slots.index((-1, dz)), f]
            after = packs[slots.index((1, dz)), f]
            beside = jnp.where(lane < lanes // 2, after, before)
            return jnp.where(inside, here, pltpu.roll(beside, lanes // 2, 1))

        mine = whole(0)
        dzs = span_offsets(spans)
        left = whole(dzs[0]) if dzs else mine
        right = left if len(dzs) < 2 else whole(dzs[1])
        return jnp.where(left_part, left, mine), jnp.where(left_part, mine, right)

    def build_strips(f, carry):
        for s, value in enumerate(strip_pair(f)):
            strips[0][f, s] = value
        return carry

    lax.fori_loop(0, fields, build_strips, 0)
    us, ws, gs = (strip_pair(fields + i) for i in range(3))
    for s in range(2):
        for i, value in enumerate(cooked(us[s], ws[s]) + (gs[s],)):
            strip_coef[i, s] = value

    def walls(v):
        up = jnp.where(row < 7, pltpu.roll(v, 7, 0), 0.0)
        down = jnp.where(row > 0, pltpu.roll(v, 1, 0), 0.0)
        return up + down

    def read(k, f, x):
        return ext[f, x] if k == 0 else states[k - 1][f, x]

    writes = []
    for k in range(steps):
        lo, hi = 1 + k, planes + 2 * DEEP - 1 - k

        def field_pair(h, carry, k=k, lo=lo, hi=hi):
            pair = [2 * h, 2 * h + 1]
            weights = [[mix[f, g] for g in range(fields)] for f in pair]
            edges = [
                jnp.where(lane % WIDE == DEEP - 1, strips[k][f, 0],
                          pltpu.roll(strips[k][f, 1], lanes - 2, 1))
                for f in pair
            ]
            for x in range(lo, hi):
                vs = [read(k, g, x) for g in range(fields)]
                c0, c1, c2, c3 = (coef[i, x] for i in range(4))
                gain_here = ext[fields + 2, x]
                for f, weight, edge in zip(pair, weights, edges):
                    mixed = total(a * v for a, v in zip(weight, vs))
                    v = read(k, f, x)
                    rim = pltpu.roll(edge, (2 * lanes - (WIDE * x + DEEP - 1)) % lanes, 1)
                    ahead = jnp.where(lane == lanes - 1, rim, pltpu.roll(v, lanes - 1, 1))
                    behind = jnp.where(lane == 0, rim, pltpu.roll(v, 1, 1))
                    states[k][f, x] = (
                        (c0 * read(k, f, x + 1) + c1 * read(k, f, x - 1))
                        + (c2 * ahead + c3 * behind)
                        + (0.05 * walls(v) - 0.3 * v)
                        + gain_here * mixed
                    )
            if k < steps - 1:
                for s in range(2):
                    vs = [strips[k][g, s] for g in range(fields)]
                    for f, weight in zip(pair, weights):
                        mixed = total(a * v for a, v in zip(weight, vs))
                        v = strips[k][f, s]
                        strips[k + 1][f, s] = (
                            strip_coef[0, s] * pltpu.roll(v, lanes - WIDE, 1)
                            + strip_coef[1, s] * pltpu.roll(v, WIDE, 1)
                            + strip_coef[2, s] * pltpu.roll(v, lanes - 1, 1)
                            + strip_coef[3, s] * pltpu.roll(v, 1, 1)
                            + (0.05 * walls(v) - 0.3 * v)
                            + strip_coef[4, s] * mixed
                        )
            return carry

        lax.fori_loop(0, fields // 2, field_pair, 0)
        write = pltpu.make_async_copy(states[k].at[:, own], krylov_out.at[k], out_sem.at[k])
        write.start()
        writes.append(write)

    def new_products(f, sums):
        for x in range(planes):
            b = [held[j, f, x] for j in range(m)]
            v = [states[k][f, DEEP + x] for k in range(steps)]
            terms = [b[j] * v[k] for j in range(m) for k in range(steps)]
            terms += [v[k] * v[l] for k, l in krylov_pairs]
            sums = [s + t for s, t in zip(sums, terms)]
        return sums

    new_sums = lax.fori_loop(0, fields, new_products, [zero] * first)
    count = first + len(upper)
    for i, s in enumerate(new_sums):
        rows[pl.ds(i, 1)] = jnp.sum(s, axis=0, keepdims=True)
    for i in range(first, count):
        rows[pl.ds(i, 1)] = jnp.sum(acc[i], axis=0, keepdims=True)
    for i in range(count, rows.shape[0]):
        rows[pl.ds(i, 1)] = jnp.zeros((1, lanes), jnp.float32)
    sums = jnp.sum(rows[...], axis=1, keepdims=True)
    at = lax.broadcasted_iota(jnp.int32, rows.shape, 0)
    spot = lax.broadcasted_iota(jnp.int32, rows.shape, 1)
    local = jnp.sum(jnp.where(at == spot, sums, 0.0), axis=0, keepdims=True)

    def summed(value, gathered, index, size, other, i):
        if size == 1:
            return value
        gathered[index] = value
        for d in range(1, size):
            pltpu.make_async_remote_copy(
                src_ref=gathered.at[index], dst_ref=gathered.at[index],
                send_sem=row_send.at[i], recv_sem=row_recv.at[i],
                device_id=other(d), device_id_type=MESH,
            ).start()
        others = gathered.at[pl.ds(0, size - 1)]
        everyone = pltpu.make_async_remote_copy(
            src_ref=others, dst_ref=others, send_sem=row_send.at[i], recv_sem=row_recv.at[i],
            device_id=other(1), device_id_type=MESH,
        )
        everyone.wait_recv()
        rows_sent.append(everyone)
        return jnp.sum(gathered[...], axis=0)

    rows_sent = []
    close = summed(local, near_rows, near_index, near_group, near_device, 0)
    sums_out[...] = summed(close, far_rows, far_index, far, far_device, 1)
    for copy in rows_sent:
        copy.wait_send()
    for copy in sends:
        copy.wait_send()
    for write in writes:
        write.wait()


def finish_kernel(
    ntot, chunks,
    sums, basis, krylov,
    proj_out, rfactor_out, new_out,
    result, out_sem,
):
    m, fields, planes = basis.shape[0], basis.shape[1], basis.shape[2]
    steps = krylov.shape[0]
    part = fields // chunks

    def piece(c):
        return pl.ds(c * part, part)

    shape = (8, basis.shape[4])
    row = sums[...] * (1.0 / ntot)

    def value(i):
        return jnp.broadcast_to(row[:, i : i + 1], shape)

    p = [[value(steps * j + k) for k in range(steps)] for j in range(m)]
    at = m * steps
    kk, bb = {}, {}
    for k in range(steps):
        for l in range(k, steps):
            kk[k, l] = value(at)
            at += 1
    for i in range(m):
        for j in range(i, m):
            bb[i, j] = bb[j, i] = value(at)
            at += 1
    q = [
        [2.0 * p[i][l] - total(bb[i, j] * p[j][l] for j in range(m)) for l in range(steps)]
        for i in range(m)
    ]
    low, inverse = {}, []
    for l in range(steps):
        for k in range(l, steps):
            g = kk[l, k] - total(p[i][l] * q[i][k] for i in range(m))
            for j in range(l):
                g = g - low[k, j] * low[l, j]
            if k == l:
                low[l, l] = jnp.sqrt(g)
                inverse.append(1.0 / low[l, l])
            else:
                low[k, l] = g * inverse[l]

    x = lax.broadcasted_iota(jnp.int32, shape, 0)
    y = lax.broadcasted_iota(jnp.int32, shape, 1)
    proj = jnp.zeros(shape, jnp.float32)
    for j in range(m):
        for k in range(steps):
            proj = jnp.where((x == j) & (y == k), p[j][k], proj)
    proj_out[...] = proj[:m, :steps]
    factor = jnp.zeros(shape, jnp.float32)
    for k, l in low:
        factor = jnp.where((x == l) & (y == k), low[k, l], factor)
    rfactor_out[...] = factor[:steps, :steps]

    writes = []
    for c in range(chunks):
        def one(i, carry, c=c):
            f = c * part + i
            for s in range(planes):
                b = [basis[j, f, s] for j in range(m)]
                done = []
                for k in range(steps):
                    v = krylov[k, f, s] - total(p[j][k] * b[j] for j in range(m))
                    for l in range(k):
                        v = v - low[k, l] * done[l]
                    done.append(v * inverse[k])
                    result[k, f, s] = done[k]
            return carry

        lax.fori_loop(0, part, one, 0)
        write = pltpu.make_async_copy(
            result.at[:, piece(c)], new_out.at[:, piece(c)], out_sem.at[c]
        )
        write.start()
        writes.append(write)
    for write in writes:
        write.wait()


def on_device(streams, spans, basis, coeffs, mixing_matrix, base_speed, span_speed, polymer_gain):
    m, fields, planes, height, lanes = basis.shape
    n = streams * spans
    near, far = near_and_far(streams)
    f32 = jnp.float32
    deep = planes + 2 * DEEP
    count = m * STEPS + STEPS * (STEPS + 1) // 2 + m * (m + 1) // 2
    padded = -(-count // 8) * 8
    links = 2 + len(partners(spans))
    hbm = pl.BlockSpec(memory_space=pltpu.HBM)
    anywhere = pl.BlockSpec(memory_space=pl.ANY)
    vmem = pl.BlockSpec(memory_space=pltpu.VMEM)
    vector = (fields, planes, height, lanes)
    krylov, sums = pl.pallas_call(
        functools.partial(krylov_kernel, streams, spans),
        out_shape=(
            jax.ShapeDtypeStruct((STEPS,) + vector, f32),
            jax.ShapeDtypeStruct((1, lanes), f32),
        ),
        in_specs=[hbm] * 6,
        out_specs=(anywhere, vmem),
        scratch_shapes=[
            pltpu.VMEM((fields + 3, deep, height, lanes), f32),
            [pltpu.VMEM((fields, deep, height, lanes), f32)] * STEPS,
            pltpu.VMEM((m,) + vector, f32),
            pltpu.VMEM((fields + 3, height, lanes), f32),
            pltpu.VMEM((links - 2, fields + 3, height, lanes), f32),
            [pltpu.VMEM((fields, 2, height, lanes), f32)] * STEPS,
            pltpu.VMEM((4, deep, height, lanes), f32),
            pltpu.VMEM((5, 2, height, lanes), f32),
            pltpu.VMEM((count, height, lanes), f32),
            pltpu.VMEM((padded, lanes), f32),
            pltpu.VMEM((near * spans, 1, lanes), f32),
            pltpu.VMEM((far, 1, lanes), f32),
            pltpu.SMEM(coeffs.shape, f32),
            pltpu.SMEM(mixing_matrix.shape, f32),
            pltpu.SemaphoreType.DMA((m + 5,)),
            pltpu.SemaphoreType.DMA((STEPS,)),
            pltpu.SemaphoreType.DMA((links,)),
            pltpu.SemaphoreType.DMA((links,)),
            pltpu.SemaphoreType.DMA((2,)),
            pltpu.SemaphoreType.DMA((2,)),
        ],
        compiler_params=pltpu.CompilerParams(
            collective_id=0, has_side_effects=True, vmem_limit_bytes=24 * 2**20
        ),
        name="krylov",
    )(*(
        pltpu.with_memory_space_constraint(x, pltpu.HBM)
        for x in (coeffs, mixing_matrix, basis, base_speed, span_speed, polymer_gain)
    ))
    chunks = 5 if fields % 5 == 0 else 1
    return pl.pallas_call(
        functools.partial(finish_kernel, float(m and basis[0].size * n), chunks),
        out_shape=(
            jax.ShapeDtypeStruct((m, STEPS), f32),
            jax.ShapeDtypeStruct((STEPS, STEPS), f32),
            jax.ShapeDtypeStruct((STEPS,) + vector, f32),
        ),
        in_specs=[vmem, vmem, vmem],
        out_specs=(vmem, vmem, hbm),
        scratch_shapes=[
            pltpu.VMEM((STEPS,) + vector, f32),
            pltpu.SemaphoreType.DMA((chunks,)),
        ],
        compiler_params=pltpu.CompilerParams(vmem_limit_bytes=24 * 2**20),
        name="finish",
    )(sums, basis, krylov)


def solution(mesh):
    placed = (
        P(None, None, "stream", None, "span"),
        P(),
        P(),
        P("stream", None, "span"),
        P("stream", None, "span"),
        P("stream", None, "span"),
    )
    return jax.shard_map(
        functools.partial(on_device, mesh.shape["stream"], mesh.shape["span"]),
        mesh=mesh,
        in_specs=placed,
        out_specs=(P(), P(), P(None, None, "stream", None, "span")),
        check_vma=False,
    )
```

```python
import functools

import jax
import jax.numpy as jnp
from jax import lax
from jax.experimental import pallas as pl
from jax.experimental.pallas import tpu as pltpu
from jax.sharding import PartitionSpec as P

STEPS = 4
DEEP = 4
WIDE = 2 * DEEP
MESH = pl.DeviceIdType.MESH


def total(terms):
    terms = list(terms)
    while len(terms) > 1:
        pairs = [terms[i] + terms[i + 1] for i in range(0, len(terms) - 1, 2)]
        terms = pairs + terms[len(terms) - len(terms) % 2 :]
    return terms[0]


def span_offsets(span):
    return () if span == 1 else ((1,) if span == 2 else (-1, 1))


def partners(span):
    dzs = span_offsets(span)
    return [(dx, 0) for dx in (-1, 1)] + [(0, dz) for dz in dzs] + [
        (dx, dz) for dx in (-1, 1) for dz in dzs
    ]


def near_and_far(streams):
    near = 16 if streams % 16 == 0 else 1
    return near, streams // near


def krylov_kernel(
    streams, spans,
    coeffs_in, mix_in, basis, base, span_speed, gain,
    krylov_out, sums_out,
    ext, states, held, pack, packs, edge, edges_in, strips, rim_rows, coef, strip_coef, acc, rows, near_rows, far_rows, coeffs, mix,
    in_sem, out_sem, send_sem, recv_sem, plane_send, plane_recv, row_send, row_recv,
):
    m, fields, planes = basis.shape[0], basis.shape[1], basis.shape[2]
    steps = STEPS
    lanes = basis.shape[4]
    sx, sz = lax.axis_index("stream"), lax.axis_index("span")
    near, far = near_and_far(streams)
    near_group = near * spans
    place = lax.rem(sx, near)
    near_index, far_index = place * spans + sz, sx // near

    def near_device(d):
        other = lax.rem(near_index + d, near_group)
        return (sx - place + other // spans, lax.rem(other, spans))

    def far_device(d):
        return (lax.rem(far_index + d, far) * near + place, sz)

    def device(dx, dz):
        return (lax.rem(sx + dx + streams, streams), lax.rem(sz + dz + spans, spans))

    barrier = pltpu.get_barrier_semaphore()

    own = pl.ds(DEEP, planes)
    loads = [
        pltpu.make_async_copy(basis.at[j], held.at[j], in_sem.at[j]) for j in range(m)
    ] + [
        pltpu.make_async_copy(ref, ext.at[fields + i, own], in_sem.at[m + i])
        for i, ref in enumerate((base, span_speed, gain))
    ] + [
        pltpu.make_async_copy(coeffs_in, coeffs, in_sem.at[m + 3]),
        pltpu.make_async_copy(mix_in, mix, in_sem.at[m + 4]),
    ]
    for load in loads:
        load.start()
    slots = partners(spans)
    greeted = [near_device(d) for d in range(1, near_group)]
    greeted += [far_device(d) for d in range(1, far)]
    if far > 1:
        greeted += [device(dx, dz) for dx, dz in slots]
    for other in greeted:
        pl.semaphore_signal(barrier, inc=1, device_id=other, device_id_type=MESH)

    lane = lax.broadcasted_iota(jnp.int32, (8, lanes), 1)
    row = lax.broadcasted_iota(jnp.int32, (8, lanes), 0)

    def packed(field, values):
        out = jnp.zeros((8, lanes), jnp.float32)
        for x in range(planes):
            at = WIDE * (x + DEEP)
            moved = pltpu.roll(values[x], DEEP + at, 1)
            out = jnp.where((lane >= at) & (lane < at + WIDE), moved, out)
        pack[field] = out

    sends, plane_sends = [], []

    def send(src, dst, dx, dz):
        i = len(sends)
        copy = pltpu.make_async_remote_copy(
            src_ref=src, dst_ref=dst, send_sem=send_sem.at[i], recv_sem=recv_sem.at[i],
            device_id=device(dx, dz), device_id_type=MESH,
        )
        copy.start()
        sends.append(copy)
        return copy

    for load in loads[m:]:
        load.wait()
    pl.semaphore_wait(barrier, len(greeted))
    third = pl.ds(fields, 3)
    send(ext.at[third, pl.ds(planes + 1, DEEP - 1)], ext.at[third, pl.ds(1, DEEP - 1)], 1, 0)
    send(ext.at[third, pl.ds(DEEP, DEEP - 1)], ext.at[third, pl.ds(planes + DEEP, DEEP - 1)], -1, 0)
    for i in range(3):
        packed(fields + i, [ext[fields + i, DEEP + x] for x in range(planes)])
    for load in loads[:m]:
        load.wait()
    weights = [coeffs[j] for j in range(m)]

    def start_field(f, carry):
        values = [total(weights[j] * held[j, f, x] for j in range(m)) for x in range(planes)]
        for x in range(planes):
            ext[f, DEEP + x] = values[x]
        packed(f, values)
        return carry

    lax.fori_loop(0, fields, start_field, 0)

    half = DEEP * WIDE
    per = lanes // half
    tops = planes * WIDE
    for e, begin in enumerate((half, tops)):
        for t in range(edge.shape[1]):
            out = jnp.zeros((8, lanes), jnp.float32)
            for j in range(per):
                f = t * per + j
                if f < fields + 3:
                    moved = pltpu.roll(pack[f], (j * half - begin) % lanes, 1)
                    out = jnp.where((lane >= j * half) & (lane < (j + 1) * half), moved, out)
            edge[e, t] = out
    for i, (dx, dz) in enumerate(slots):
        if dx == 0:
            send(pack, packs.at[i - 2], -dx, -dz)
    corner = [slot for slot in slots if slot[0] != 0]
    for i, (dx, dz) in enumerate(corner):
        send(edge.at[1 if dx == -1 else 0], edges_in.at[i], -dx, -dz)
    main = pl.ds(0, fields)
    for d in range(DEEP):
        pair = []
        for side, (src, dst) in enumerate((
            (planes + DEEP - 1 - d, DEEP - 1 - d), (DEEP + d, planes + DEEP + d)
        )):
            copy = pltpu.make_async_remote_copy(
                src_ref=ext.at[main, src], dst_ref=ext.at[main, dst],
                send_sem=plane_send.at[2 * d + side], recv_sem=plane_recv.at[2 * d + side],
                device_id=device(1 - 2 * side, 0), device_id_type=MESH,
            )
            copy.start()
            pair.append(copy)
        plane_sends.append(pair)

    upper = [(i, j) for i in range(m) for j in range(i, m)]
    krylov_pairs = [(k, l) for k in range(steps) for l in range(k, steps)]
    zero = jnp.zeros((8, lanes), jnp.float32)

    def basis_products(f, sums):
        for x in range(planes):
            b = [held[j, f, x] for j in range(m)]
            sums = [s + b[i] * b[j] for s, (i, j) in zip(sums, upper)]
        return sums

    basis_sums = lax.fori_loop(0, fields, basis_products, [zero] * len(upper))
    first = m * steps + len(krylov_pairs)
    for i, s in enumerate(basis_sums):
        acc[first + i] = s

    for copy in sends:
        copy.wait_recv()

    def cooked(u, w):
        return (
            0.05 - 0.5 * u, 0.05 + 0.5 * u, 0.05 - 0.5 * w, 0.05 + 0.5 * w
        )

    for x in range(1, planes + 2 * DEEP - 1):
        for i, value in enumerate(cooked(ext[fields, x], ext[fields + 1, x])):
            coef[i, x] = value

    inside = (lane >= half) & (lane < half + planes * WIDE)
    left_part = lane % WIDE < DEEP

    def strip_pair(f):
        tile, spot = f // per, f % per

        def whole(dz):
            here = pack[f] if dz == 0 else packs[slots.index((0, dz)) - 2, f]
            before = edges_in[corner.index((-1, dz)), tile]
            after = edges_in[corner.index((1, dz)), tile]
            before = pltpu.roll(before, (-spot * half) % lanes, 1)
            after = pltpu.roll(after, (tops + half - spot * half) % lanes, 1)
            return jnp.where(inside, here, jnp.where(lane < half, before, after))

        mine = whole(0)
        dzs = span_offsets(spans)
        left = whole(dzs[0]) if dzs else mine
        right = left if len(dzs) < 2 else whole(dzs[1])
        return jnp.where(left_part, left, mine), jnp.where(left_part, mine, right)

    for f in range(fields):
        for s, value in enumerate(strip_pair(f)):
            strips[0][f, s] = value
    us, ws, gs = (strip_pair(fields + i) for i in range(3))
    for s in range(2):
        for i, value in enumerate(cooked(us[s], ws[s]) + (gs[s],)):
            strip_coef[i, s] = value

    def walls(v):
        up = jnp.where(row < 7, pltpu.roll(v, 7, 0), 0.0)
        down = jnp.where(row > 0, pltpu.roll(v, 1, 0), 0.0)
        return up + down

    def read(k, f, x):
        return ext[f, x] if k == 0 else states[k - 1][f, x]

    def strip_step(k):
        def field(f, carry):
            weight = [mix[f, g] for g in range(fields)]
            for s in range(2):
                mixed = total(a * strips[k][g, s] for g, a in enumerate(weight))
                v = strips[k][f, s]
                strips[k + 1][f, s] = (
                    strip_coef[0, s] * pltpu.roll(v, lanes - WIDE, 1)
                    + strip_coef[1, s] * pltpu.roll(v, WIDE, 1)
                    + strip_coef[2, s] * pltpu.roll(v, lanes - 1, 1)
                    + strip_coef[3, s] * pltpu.roll(v, 1, 1)
                    + (0.05 * walls(v) - 0.3 * v)
                    + strip_coef[4, s] * mixed
                )
            return carry

        lax.fori_loop(0, fields, field, 0, unroll=2 if fields % 2 == 0 else 1)

    def rims(k):
        def field(f, carry):
            rim_rows[k][f] = jnp.where(
                lane % WIDE == DEEP - 1, strips[k][f, 0],
                pltpu.roll(strips[k][f, 1], lanes - 2, 1),
            )
            return carry

        lax.fori_loop(0, fields, field, 0, unroll=2 if fields % 2 == 0 else 1)

    def advance(k, which, group):
        if not which:
            return

        def field_group(h, carry):
            some = [group * h + i for i in range(group)]
            weights = [[mix[f, g] for g in range(fields)] for f in some]
            sides = [rim_rows[k][f] for f in some]
            for x in which:
                vs = [read(k, g, x) for g in range(fields)]
                c0, c1, c2, c3 = (coef[i, x] for i in range(4))
                gain_here = ext[fields + 2, x]
                for f, weight, side in zip(some, weights, sides):
                    mixed = total(a * v for a, v in zip(weight, vs))
                    v = read(k, f, x)
                    rim = pltpu.roll(side, (2 * lanes - (WIDE * x + DEEP - 1)) % lanes, 1)
                    ahead = jnp.where(lane == lanes - 1, rim, pltpu.roll(v, lanes - 1, 1))
                    behind = jnp.where(lane == 0, rim, pltpu.roll(v, 1, 1))
                    states[k][f, x] = (
                        (c0 * read(k, f, x + 1) + c1 * read(k, f, x - 1))
                        + (c2 * ahead + c3 * behind)
                        + (0.05 * walls(v) - 0.3 * v)
                        + gain_here * mixed
                    )
            return carry

        lax.fori_loop(0, fields // group, field_group, 0)

    for k in range(steps):
        rims(k)
        if k < steps - 1:
            strip_step(k)
    pair_size = 2 if fields % 2 == 0 else 1
    large = 5 if fields % 5 == 0 else 1
    last = DEEP + planes
    for k in range(steps):
        advance(k, range(DEEP + 1 + k, last - 1 - k), pair_size)
    writes = []
    for d in range(1, DEEP + 1):
        for copy in plane_sends[d - 1]:
            copy.wait_recv()
        for k in range(steps):
            advance(k, sorted({DEEP + 1 + k - d, last - 2 - k + d}), large)
            if d == DEEP:
                write = pltpu.make_async_copy(
                    states[k].at[:, own], krylov_out.at[k], out_sem.at[k]
                )
                write.start()
                writes.append(write)

    def new_products(f, sums):
        for x in range(planes):
            b = [held[j, f, x] for j in range(m)]
            v = [states[k][f, DEEP + x] for k in range(steps)]
            terms = [b[j] * v[k] for j in range(m) for k in range(steps)]
            terms += [v[k] * v[l] for k, l in krylov_pairs]
            sums = [s + t for s, t in zip(sums, terms)]
        return sums

    new_sums = lax.fori_loop(0, fields, new_products, [zero] * first)
    count = first + len(upper)
    for i, s in enumerate(new_sums):
        rows[pl.ds(i, 1)] = jnp.sum(s, axis=0, keepdims=True)
    for i in range(first, count):
        rows[pl.ds(i, 1)] = jnp.sum(acc[i], axis=0, keepdims=True)
    for i in range(count, rows.shape[0]):
        rows[pl.ds(i, 1)] = jnp.zeros((1, lanes), jnp.float32)
    sums = jnp.sum(rows[...], axis=1, keepdims=True)
    at = lax.broadcasted_iota(jnp.int32, rows.shape, 0)
    spot = lax.broadcasted_iota(jnp.int32, rows.shape, 1)
    local = jnp.sum(jnp.where(at == spot, sums, 0.0), axis=0, keepdims=True)

    def summed(value, gathered, index, size, other, i):
        if size == 1:
            return value
        gathered[index] = value
        for d in range(1, size):
            pltpu.make_async_remote_copy(
                src_ref=gathered.at[index], dst_ref=gathered.at[index],
                send_sem=row_send.at[i], recv_sem=row_recv.at[i],
                device_id=other(d), device_id_type=MESH,
            ).start()
        others = gathered.at[pl.ds(0, size - 1)]
        everyone = pltpu.make_async_remote_copy(
            src_ref=others, dst_ref=others, send_sem=row_send.at[i], recv_sem=row_recv.at[i],
            device_id=other(1), device_id_type=MESH,
        )
        everyone.wait_recv()
        rows_sent.append(everyone)
        return jnp.sum(gathered[...], axis=0)

    rows_sent = []
    close = summed(local, near_rows, near_index, near_group, near_device, 0)
    sums_out[...] = summed(close, far_rows, far_index, far, far_device, 1)
    for copy in rows_sent:
        copy.wait_send()
    for copy in sends + [copy for pair in plane_sends for copy in pair]:
        copy.wait_send()
    for write in writes:
        write.wait()


def finish_kernel(
    ntot, chunks,
    sums, basis, krylov,
    proj_out, rfactor_out, new_out,
    result, out_sem,
):
    m, fields, planes = basis.shape[0], basis.shape[1], basis.shape[2]
    steps = krylov.shape[0]
    part = fields // chunks

    def piece(c):
        return pl.ds(c * part, part)

    shape = (8, basis.shape[4])
    row = sums[...] * (1.0 / ntot)

    def value(i):
        return jnp.broadcast_to(row[:, i : i + 1], shape)

    p = [[value(steps * j + k) for k in range(steps)] for j in range(m)]
    at = m * steps
    kk, bb = {}, {}
    for k in range(steps):
        for l in range(k, steps):
            kk[k, l] = value(at)
            at += 1
    for i in range(m):
        for j in range(i, m):
            bb[i, j] = bb[j, i] = value(at)
            at += 1
    q = [
        [2.0 * p[i][l] - total(bb[i, j] * p[j][l] for j in range(m)) for l in range(steps)]
        for i in range(m)
    ]
    low, inverse = {}, []
    for l in range(steps):
        for k in range(l, steps):
            g = kk[l, k] - total(p[i][l] * q[i][k] for i in range(m))
            for j in range(l):
                g = g - low[k, j] * low[l, j]
            if k == l:
                low[l, l] = jnp.sqrt(g)
                inverse.append(1.0 / low[l, l])
            else:
                low[k, l] = g * inverse[l]

    x = lax.broadcasted_iota(jnp.int32, shape, 0)
    y = lax.broadcasted_iota(jnp.int32, shape, 1)
    proj = jnp.zeros(shape, jnp.float32)
    for j in range(m):
        for k in range(steps):
            proj = jnp.where((x == j) & (y == k), p[j][k], proj)
    proj_out[...] = proj[:m, :steps]
    factor = jnp.zeros(shape, jnp.float32)
    for k, l in low:
        factor = jnp.where((x == l) & (y == k), low[k, l], factor)
    rfactor_out[...] = factor[:steps, :steps]

    writes = []
    for c in range(chunks):
        def one(i, carry, c=c):
            f = c * part + i
            for s in range(planes):
                b = [basis[j, f, s] for j in range(m)]
                done = []
                for k in range(steps):
                    v = krylov[k, f, s] - total(p[j][k] * b[j] for j in range(m))
                    for l in range(k):
                        v = v - low[k, l] * done[l]
                    done.append(v * inverse[k])
                    result[k, f, s] = done[k]
            return carry

        lax.fori_loop(0, part, one, 0)
        write = pltpu.make_async_copy(
            result.at[:, piece(c)], new_out.at[:, piece(c)], out_sem.at[c]
        )
        write.start()
        writes.append(write)
    for write in writes:
        write.wait()


def on_device(streams, spans, basis, coeffs, mixing_matrix, base_speed, span_speed, polymer_gain):
    m, fields, planes, height, lanes = basis.shape
    n = streams * spans
    near, far = near_and_far(streams)
    f32 = jnp.float32
    deep = planes + 2 * DEEP
    count = m * STEPS + STEPS * (STEPS + 1) // 2 + m * (m + 1) // 2
    padded = -(-count // 8) * 8
    links = 2 + len(partners(spans))
    spans_beside = len(span_offsets(spans))
    corners = 2 + 2 * spans_beside
    tiles = -(-(fields + 3) * DEEP * WIDE // lanes)
    hbm = pl.BlockSpec(memory_space=pltpu.HBM)
    anywhere = pl.BlockSpec(memory_space=pl.ANY)
    vmem = pl.BlockSpec(memory_space=pltpu.VMEM)
    vector = (fields, planes, height, lanes)
    krylov, sums = pl.pallas_call(
        functools.partial(krylov_kernel, streams, spans),
        out_shape=(
            jax.ShapeDtypeStruct((STEPS,) + vector, f32),
            jax.ShapeDtypeStruct((1, lanes), f32),
        ),
        in_specs=[hbm] * 6,
        out_specs=(anywhere, vmem),
        scratch_shapes=[
            pltpu.VMEM((fields + 3, deep, height, lanes), f32),
            [pltpu.VMEM((fields, deep, height, lanes), f32)] * STEPS,
            pltpu.VMEM((m,) + vector, f32),
            pltpu.VMEM((fields + 3, height, lanes), f32),
            pltpu.VMEM((max(spans_beside, 1), fields + 3, height, lanes), f32),
            pltpu.VMEM((2, tiles, height, lanes), f32),
            pltpu.VMEM((corners, tiles, height, lanes), f32),
            [pltpu.VMEM((fields, 2, height, lanes), f32)] * STEPS,
            [pltpu.VMEM((fields, height, lanes), f32)] * STEPS,
            pltpu.VMEM((4, deep, height, lanes), f32),
            pltpu.VMEM((5, 2, height, lanes), f32),
            pltpu.VMEM((count, height, lanes), f32),
            pltpu.VMEM((padded, lanes), f32),
            pltpu.VMEM((near * spans, 1, lanes), f32),
            pltpu.VMEM((far, 1, lanes), f32),
            pltpu.SMEM(coeffs.shape, f32),
            pltpu.SMEM(mixing_matrix.shape, f32),
            pltpu.SemaphoreType.DMA((m + 5,)),
            pltpu.SemaphoreType.DMA((STEPS,)),
            pltpu.SemaphoreType.DMA((links,)),
            pltpu.SemaphoreType.DMA((links,)),
            pltpu.SemaphoreType.DMA((2 * DEEP,)),
            pltpu.SemaphoreType.DMA((2 * DEEP,)),
            pltpu.SemaphoreType.DMA((2,)),
            pltpu.SemaphoreType.DMA((2,)),
        ],
        compiler_params=pltpu.CompilerParams(
            collective_id=0, has_side_effects=True, vmem_limit_bytes=24 * 2**20
        ),
        name="krylov",
    )(*(
        pltpu.with_memory_space_constraint(x, pltpu.HBM)
        for x in (coeffs, mixing_matrix, basis, base_speed, span_speed, polymer_gain)
    ))
    chunks = 5 if fields % 5 == 0 else 1
    return pl.pallas_call(
        functools.partial(finish_kernel, float(m and basis[0].size * n), chunks),
        out_shape=(
            jax.ShapeDtypeStruct((m, STEPS), f32),
            jax.ShapeDtypeStruct((STEPS, STEPS), f32),
            jax.ShapeDtypeStruct((STEPS,) + vector, f32),
        ),
        in_specs=[vmem, vmem, vmem],
        out_specs=(vmem, vmem, hbm),
        scratch_shapes=[
            pltpu.VMEM((STEPS,) + vector, f32),
            pltpu.SemaphoreType.DMA((chunks,)),
        ],
        compiler_params=pltpu.CompilerParams(vmem_limit_bytes=24 * 2**20),
        name="finish",
    )(sums, basis, krylov)


def solution(mesh):
    placed = (
        P(None, None, "stream", None, "span"),
        P(),
        P(),
        P("stream", None, "span"),
        P("stream", None, "span"),
        P("stream", None, "span"),
    )
    return jax.shard_map(
        functools.partial(on_device, mesh.shape["stream"], mesh.shape["span"]),
        mesh=mesh,
        in_specs=placed,
        out_specs=(P(), P(), P(None, None, "stream", None, "span")),
        check_vma=False,
    )
```

```python
import functools

import jax
import jax.numpy as jnp
from jax import lax
from jax.experimental import pallas as pl
from jax.experimental.pallas import tpu as pltpu
from jax.sharding import PartitionSpec as P

STEPS = 4
DEEP = 4
WIDE = 2 * DEEP
MESH = pl.DeviceIdType.MESH


def total(terms):
    terms = list(terms)
    while len(terms) > 1:
        pairs = [terms[i] + terms[i + 1] for i in range(0, len(terms) - 1, 2)]
        terms = pairs + terms[len(terms) - len(terms) % 2 :]
    return terms[0]


def span_offsets(span):
    return () if span == 1 else ((1,) if span == 2 else (-1, 1))


def partners(span):
    dzs = span_offsets(span)
    return [(dx, 0) for dx in (-1, 1)] + [(0, dz) for dz in dzs] + [
        (dx, dz) for dx in (-1, 1) for dz in dzs
    ]


def near_and_far(streams):
    near = 16 if streams % 16 == 0 else 1
    return near, streams // near


def krylov_kernel(
    streams, spans,
    coeffs_in, mix_in, basis, base, span_speed, gain,
    krylov_out, sums_out,
    ext, states, held, pack, packs, edge, edges_in, strips, rim_rows, coef, strip_coef, acc, rows, near_rows, far_rows, coeffs, mix,
    in_sem, out_sem, send_sem, recv_sem, plane_send, plane_recv, row_send, row_recv,
):
    m, fields, planes = basis.shape[0], basis.shape[1], basis.shape[2]
    steps = STEPS
    lanes = basis.shape[4]
    sx, sz = lax.axis_index("stream"), lax.axis_index("span")
    near, far = near_and_far(streams)
    near_group = near * spans
    place = lax.rem(sx, near)
    near_index, far_index = place * spans + sz, sx // near

    def near_device(d):
        other = lax.rem(near_index + d, near_group)
        return (sx - place + other // spans, lax.rem(other, spans))

    def far_device(d):
        return (lax.rem(far_index + d, far) * near + place, sz)

    def device(dx, dz):
        return (lax.rem(sx + dx + streams, streams), lax.rem(sz + dz + spans, spans))

    barrier = pltpu.get_barrier_semaphore()

    own = pl.ds(DEEP, planes)
    loads = [
        pltpu.make_async_copy(basis.at[j], held.at[j], in_sem.at[j]) for j in range(m)
    ] + [
        pltpu.make_async_copy(ref, ext.at[fields + i, own], in_sem.at[m + i])
        for i, ref in enumerate((base, span_speed, gain))
    ] + [
        pltpu.make_async_copy(coeffs_in, coeffs, in_sem.at[m + 3]),
        pltpu.make_async_copy(mix_in, mix, in_sem.at[m + 4]),
    ]
    for load in loads:
        load.start()
    slots = partners(spans)
    greeted = [near_device(d) for d in range(1, near_group)]
    greeted += [far_device(d) for d in range(1, far)]
    if far > 1:
        greeted += [device(dx, dz) for dx, dz in slots]
    for other in greeted:
        pl.semaphore_signal(barrier, inc=1, device_id=other, device_id_type=MESH)

    lane = lax.broadcasted_iota(jnp.int32, (8, lanes), 1)
    row = lax.broadcasted_iota(jnp.int32, (8, lanes), 0)

    def packed(field, values):
        out = jnp.zeros((8, lanes), jnp.float32)
        for x in range(planes):
            at = WIDE * (x + DEEP)
            moved = pltpu.roll(values[x], DEEP + at, 1)
            out = jnp.where((lane >= at) & (lane < at + WIDE), moved, out)
        pack[field] = out

    sends, plane_sends = [], []

    def send(src, dst, dx, dz):
        i = len(sends)
        copy = pltpu.make_async_remote_copy(
            src_ref=src, dst_ref=dst, send_sem=send_sem.at[i], recv_sem=recv_sem.at[i],
            device_id=device(dx, dz), device_id_type=MESH,
        )
        copy.start()
        sends.append(copy)
        return copy

    for load in loads[m:]:
        load.wait()
    pl.semaphore_wait(barrier, len(greeted))
    third = pl.ds(fields, 3)
    send(ext.at[third, pl.ds(planes + 1, DEEP - 1)], ext.at[third, pl.ds(1, DEEP - 1)], 1, 0)
    send(ext.at[third, pl.ds(DEEP, DEEP - 1)], ext.at[third, pl.ds(planes + DEEP, DEEP - 1)], -1, 0)
    for i in range(3):
        packed(fields + i, [ext[fields + i, DEEP + x] for x in range(planes)])
    for load in loads[:m]:
        load.wait()
    weights = [coeffs[j] for j in range(m)]

    def start_field(f, carry):
        values = [total(weights[j] * held[j, f, x] for j in range(m)) for x in range(planes)]
        for x in range(planes):
            ext[f, DEEP + x] = values[x]
        packed(f, values)
        return carry

    lax.fori_loop(0, fields, start_field, 0)

    half = DEEP * WIDE
    per = lanes // half
    tops = planes * WIDE
    for e, begin in enumerate((half, tops)):
        for t in range(edge.shape[1]):
            out = jnp.zeros((8, lanes), jnp.float32)
            for j in range(per):
                f = t * per + j
                if f < fields + 3:
                    moved = pltpu.roll(pack[f], (j * half - begin) % lanes, 1)
                    out = jnp.where((lane >= j * half) & (lane < (j + 1) * half), moved, out)
            edge[e, t] = out
    for i, (dx, dz) in enumerate(slots):
        if dx == 0:
            send(pack, packs.at[i - 2], -dx, -dz)
    corner = [slot for slot in slots if slot[0] != 0]
    for i, (dx, dz) in enumerate(corner):
        send(edge.at[1 if dx == -1 else 0], edges_in.at[i], -dx, -dz)
    main = pl.ds(0, fields)
    for d in range(DEEP):
        pair = []
        for side, (src, dst) in enumerate((
            (planes + DEEP - 1 - d, DEEP - 1 - d), (DEEP + d, planes + DEEP + d)
        )):
            copy = pltpu.make_async_remote_copy(
                src_ref=ext.at[main, src], dst_ref=ext.at[main, dst],
                send_sem=plane_send.at[2 * d + side], recv_sem=plane_recv.at[2 * d + side],
                device_id=device(1 - 2 * side, 0), device_id_type=MESH,
            )
            copy.start()
            pair.append(copy)
        plane_sends.append(pair)

    upper = [(i, j) for i in range(m) for j in range(i, m)]
    krylov_pairs = [(k, l) for k in range(steps) for l in range(k, steps)]
    zero = jnp.zeros((8, lanes), jnp.float32)

    def basis_products(f, sums):
        for x in range(planes):
            b = [held[j, f, x] for j in range(m)]
            sums = [s + b[i] * b[j] for s, (i, j) in zip(sums, upper)]
        return sums

    basis_sums = lax.fori_loop(0, fields, basis_products, [zero] * len(upper))
    first = m * steps + len(krylov_pairs)
    for i, s in enumerate(basis_sums):
        acc[first + i] = s

    for copy in sends:
        copy.wait_recv()

    def cooked(u, w):
        return (
            0.05 - 0.5 * u, 0.05 + 0.5 * u, 0.05 - 0.5 * w, 0.05 + 0.5 * w
        )

    for x in range(1, planes + 2 * DEEP - 1):
        for i, value in enumerate(cooked(ext[fields, x], ext[fields + 1, x])):
            coef[i, x] = value

    inside = (lane >= half) & (lane < half + planes * WIDE)
    left_part = lane % WIDE < DEEP

    def strip_pair(f):
        tile, spot = f // per, f % per

        def whole(dz):
            here = pack[f] if dz == 0 else packs[slots.index((0, dz)) - 2, f]
            before = edges_in[corner.index((-1, dz)), tile]
            after = edges_in[corner.index((1, dz)), tile]
            before = pltpu.roll(before, (-spot * half) % lanes, 1)
            after = pltpu.roll(after, (tops + half - spot * half) % lanes, 1)
            return jnp.where(inside, here, jnp.where(lane < half, before, after))

        mine = whole(0)
        dzs = span_offsets(spans)
        left = whole(dzs[0]) if dzs else mine
        right = left if len(dzs) < 2 else whole(dzs[1])
        return jnp.where(left_part, left, mine), jnp.where(left_part, mine, right)

    for f in range(fields):
        for s, value in enumerate(strip_pair(f)):
            strips[0][f, s] = value
    us, ws, gs = (strip_pair(fields + i) for i in range(3))
    for s in range(2):
        for i, value in enumerate(cooked(us[s], ws[s]) + (gs[s],)):
            strip_coef[i, s] = value

    def walls(v):
        up = jnp.where(row < 7, pltpu.roll(v, 7, 0), 0.0)
        down = jnp.where(row > 0, pltpu.roll(v, 1, 0), 0.0)
        return up + down

    def read(k, f, x):
        return ext[f, x] if k == 0 else states[k - 1][f, x]

    def strip_step(k):
        def field(f, carry):
            weight = [mix[f, g] for g in range(fields)]
            done = []
            for s in range(2):
                mixed = total(a * strips[k][g, s] for g, a in enumerate(weight))
                v = strips[k][f, s]
                done.append(
                    strip_coef[0, s] * pltpu.roll(v, lanes - WIDE, 1)
                    + strip_coef[1, s] * pltpu.roll(v, WIDE, 1)
                    + strip_coef[2, s] * pltpu.roll(v, lanes - 1, 1)
                    + strip_coef[3, s] * pltpu.roll(v, 1, 1)
                    + (0.05 * walls(v) - 0.3 * v)
                    + strip_coef[4, s] * mixed
                )
            for s in range(2):
                strips[k + 1][f, s] = done[s]
            return carry

        lax.fori_loop(0, fields, field, 0, unroll=2 if fields % 2 == 0 else 1)

    def rims(k):
        def field(f, carry):
            rim_rows[k][f] = jnp.where(
                lane % WIDE == DEEP - 1, strips[k][f, 0],
                pltpu.roll(strips[k][f, 1], lanes - 2, 1),
            )
            return carry

        lax.fori_loop(0, fields, field, 0, unroll=2 if fields % 2 == 0 else 1)

    def advance(k, which, group):
        if not which:
            return

        def field_group(h, carry):
            some = [group * h + i for i in range(group)]
            weights = [[mix[f, g] for g in range(fields)] for f in some]
            sides = [rim_rows[k][f] for f in some]
            done = []
            for x in which:
                vs = [read(k, g, x) for g in range(fields)]
                c0, c1, c2, c3 = (coef[i, x] for i in range(4))
                gain_here = ext[fields + 2, x]
                for f, weight, side in zip(some, weights, sides):
                    mixed = total(a * v for a, v in zip(weight, vs))
                    v = read(k, f, x)
                    rim = pltpu.roll(side, (2 * lanes - (WIDE * x + DEEP - 1)) % lanes, 1)
                    ahead = jnp.where(lane == lanes - 1, rim, pltpu.roll(v, lanes - 1, 1))
                    behind = jnp.where(lane == 0, rim, pltpu.roll(v, 1, 1))
                    done.append((f, x, (
                        (c0 * read(k, f, x + 1) + c1 * read(k, f, x - 1))
                        + (c2 * ahead + c3 * behind)
                        + (0.05 * walls(v) - 0.3 * v)
                        + gain_here * mixed
                    )))
            for f, x, value in done:
                states[k][f, x] = value
            return carry

        lax.fori_loop(0, fields // group, field_group, 0)

    for k in range(steps):
        rims(k)
        if k < steps - 1:
            strip_step(k)
    pair_size = 2 if fields % 2 == 0 else 1
    large = 5 if fields % 5 == 0 else 1
    last = DEEP + planes
    for k in range(steps):
        advance(k, range(DEEP + 1 + k, last - 1 - k), pair_size)
    writes = []
    for d in range(1, DEEP + 1):
        for copy in plane_sends[d - 1]:
            copy.wait_recv()
        for k in range(steps):
            advance(k, sorted({DEEP + 1 + k - d, last - 2 - k + d}), large)
            if d == DEEP:
                write = pltpu.make_async_copy(
                    states[k].at[:, own], krylov_out.at[k], out_sem.at[k]
                )
                write.start()
                writes.append(write)

    def new_products(f, sums):
        for x in range(planes):
            b = [held[j, f, x] for j in range(m)]
            v = [states[k][f, DEEP + x] for k in range(steps)]
            terms = [b[j] * v[k] for j in range(m) for k in range(steps)]
            terms += [v[k] * v[l] for k, l in krylov_pairs]
            sums = [s + t for s, t in zip(sums, terms)]
        return sums

    new_sums = lax.fori_loop(0, fields, new_products, [zero] * first)
    count = first + len(upper)
    for i, s in enumerate(new_sums):
        rows[pl.ds(i, 1)] = jnp.sum(s, axis=0, keepdims=True)
    for i in range(first, count):
        rows[pl.ds(i, 1)] = jnp.sum(acc[i], axis=0, keepdims=True)
    for i in range(count, rows.shape[0]):
        rows[pl.ds(i, 1)] = jnp.zeros((1, lanes), jnp.float32)
    sums = jnp.sum(rows[...], axis=1, keepdims=True)
    at = lax.broadcasted_iota(jnp.int32, rows.shape, 0)
    spot = lax.broadcasted_iota(jnp.int32, rows.shape, 1)
    local = jnp.sum(jnp.where(at == spot, sums, 0.0), axis=0, keepdims=True)

    def summed(value, gathered, index, size, other, i):
        if size == 1:
            return value
        gathered[index] = value
        for d in range(1, size):
            pltpu.make_async_remote_copy(
                src_ref=gathered.at[index], dst_ref=gathered.at[index],
                send_sem=row_send.at[i], recv_sem=row_recv.at[i],
                device_id=other(d), device_id_type=MESH,
            ).start()
        others = gathered.at[pl.ds(0, size - 1)]
        everyone = pltpu.make_async_remote_copy(
            src_ref=others, dst_ref=others, send_sem=row_send.at[i], recv_sem=row_recv.at[i],
            device_id=other(1), device_id_type=MESH,
        )
        everyone.wait_recv()
        rows_sent.append(everyone)
        return jnp.sum(gathered[...], axis=0)

    rows_sent = []
    close = summed(local, near_rows, near_index, near_group, near_device, 0)
    sums_out[...] = summed(close, far_rows, far_index, far, far_device, 1)
    for copy in rows_sent:
        copy.wait_send()
    for copy in sends + [copy for pair in plane_sends for copy in pair]:
        copy.wait_send()
    for write in writes:
        write.wait()


def finish_kernel(
    ntot, chunks,
    sums, basis, krylov,
    proj_out, rfactor_out, new_out,
    result, out_sem,
):
    m, fields, planes = basis.shape[0], basis.shape[1], basis.shape[2]
    steps = krylov.shape[0]
    part = fields // chunks

    def piece(c):
        return pl.ds(c * part, part)

    shape = (8, basis.shape[4])
    row = sums[...] * (1.0 / ntot)

    def value(i):
        return jnp.broadcast_to(row[:, i : i + 1], shape)

    p = [[value(steps * j + k) for k in range(steps)] for j in range(m)]
    at = m * steps
    kk, bb = {}, {}
    for k in range(steps):
        for l in range(k, steps):
            kk[k, l] = value(at)
            at += 1
    for i in range(m):
        for j in range(i, m):
            bb[i, j] = bb[j, i] = value(at)
            at += 1
    q = [
        [2.0 * p[i][l] - total(bb[i, j] * p[j][l] for j in range(m)) for l in range(steps)]
        for i in range(m)
    ]
    low, inverse = {}, []
    for l in range(steps):
        for k in range(l, steps):
            g = kk[l, k] - total(p[i][l] * q[i][k] for i in range(m))
            for j in range(l):
                g = g - low[k, j] * low[l, j]
            if k == l:
                low[l, l] = jnp.sqrt(g)
                inverse.append(1.0 / low[l, l])
            else:
                low[k, l] = g * inverse[l]

    x = lax.broadcasted_iota(jnp.int32, shape, 0)
    y = lax.broadcasted_iota(jnp.int32, shape, 1)
    proj = jnp.zeros(shape, jnp.float32)
    for j in range(m):
        for k in range(steps):
            proj = jnp.where((x == j) & (y == k), p[j][k], proj)
    proj_out[...] = proj[:m, :steps]
    factor = jnp.zeros(shape, jnp.float32)
    for k, l in low:
        factor = jnp.where((x == l) & (y == k), low[k, l], factor)
    rfactor_out[...] = factor[:steps, :steps]

    writes = []
    for c in range(chunks):
        def one(i, carry, c=c):
            f = c * part + i
            for half in range(0, planes, 4):
                values = []
                for s in range(half, min(half + 4, planes)):
                    b = [basis[j, f, s] for j in range(m)]
                    done = []
                    for k in range(steps):
                        v = krylov[k, f, s] - total(p[j][k] * b[j] for j in range(m))
                        for l in range(k):
                            v = v - low[k, l] * done[l]
                        done.append(v * inverse[k])
                        values.append((k, s, done[k]))
                for k, s, value in values:
                    result[k, f, s] = value
            return carry

        lax.fori_loop(0, part, one, 0)
        write = pltpu.make_async_copy(
            result.at[:, piece(c)], new_out.at[:, piece(c)], out_sem.at[c]
        )
        write.start()
        writes.append(write)
    for write in writes:
        write.wait()


def on_device(streams, spans, basis, coeffs, mixing_matrix, base_speed, span_speed, polymer_gain):
    m, fields, planes, height, lanes = basis.shape
    n = streams * spans
    near, far = near_and_far(streams)
    f32 = jnp.float32
    deep = planes + 2 * DEEP
    count = m * STEPS + STEPS * (STEPS + 1) // 2 + m * (m + 1) // 2
    padded = -(-count // 8) * 8
    links = 2 + len(partners(spans))
    spans_beside = len(span_offsets(spans))
    corners = 2 + 2 * spans_beside
    tiles = -(-(fields + 3) * DEEP * WIDE // lanes)
    hbm = pl.BlockSpec(memory_space=pltpu.HBM)
    anywhere = pl.BlockSpec(memory_space=pl.ANY)
    vmem = pl.BlockSpec(memory_space=pltpu.VMEM)
    vector = (fields, planes, height, lanes)
    krylov, sums = pl.pallas_call(
        functools.partial(krylov_kernel, streams, spans),
        out_shape=(
            jax.ShapeDtypeStruct((STEPS,) + vector, f32),
            jax.ShapeDtypeStruct((1, lanes), f32),
        ),
        in_specs=[hbm] * 6,
        out_specs=(anywhere, vmem),
        scratch_shapes=[
            pltpu.VMEM((fields + 3, deep, height, lanes), f32),
            [pltpu.VMEM((fields, deep, height, lanes), f32)] * STEPS,
            pltpu.VMEM((m,) + vector, f32),
            pltpu.VMEM((fields + 3, height, lanes), f32),
            pltpu.VMEM((max(spans_beside, 1), fields + 3, height, lanes), f32),
            pltpu.VMEM((2, tiles, height, lanes), f32),
            pltpu.VMEM((corners, tiles, height, lanes), f32),
            [pltpu.VMEM((fields, 2, height, lanes), f32)] * STEPS,
            [pltpu.VMEM((fields, height, lanes), f32)] * STEPS,
            pltpu.VMEM((4, deep, height, lanes), f32),
            pltpu.VMEM((5, 2, height, lanes), f32),
            pltpu.VMEM((count, height, lanes), f32),
            pltpu.VMEM((padded, lanes), f32),
            pltpu.VMEM((near * spans, 1, lanes), f32),
            pltpu.VMEM((far, 1, lanes), f32),
            pltpu.SMEM(coeffs.shape, f32),
            pltpu.SMEM(mixing_matrix.shape, f32),
            pltpu.SemaphoreType.DMA((m + 5,)),
            pltpu.SemaphoreType.DMA((STEPS,)),
            pltpu.SemaphoreType.DMA((links,)),
            pltpu.SemaphoreType.DMA((links,)),
            pltpu.SemaphoreType.DMA((2 * DEEP,)),
            pltpu.SemaphoreType.DMA((2 * DEEP,)),
            pltpu.SemaphoreType.DMA((2,)),
            pltpu.SemaphoreType.DMA((2,)),
        ],
        compiler_params=pltpu.CompilerParams(
            collective_id=0, has_side_effects=True, vmem_limit_bytes=24 * 2**20
        ),
        name="krylov",
    )(*(
        pltpu.with_memory_space_constraint(x, pltpu.HBM)
        for x in (coeffs, mixing_matrix, basis, base_speed, span_speed, polymer_gain)
    ))
    chunks = 5 if fields % 5 == 0 else 1
    return pl.pallas_call(
        functools.partial(finish_kernel, float(m and basis[0].size * n), chunks),
        out_shape=(
            jax.ShapeDtypeStruct((m, STEPS), f32),
            jax.ShapeDtypeStruct((STEPS, STEPS), f32),
            jax.ShapeDtypeStruct((STEPS,) + vector, f32),
        ),
        in_specs=[vmem, vmem, vmem],
        out_specs=(vmem, vmem, hbm),
        scratch_shapes=[
            pltpu.VMEM((STEPS,) + vector, f32),
            pltpu.SemaphoreType.DMA((chunks,)),
        ],
        compiler_params=pltpu.CompilerParams(vmem_limit_bytes=24 * 2**20),
        name="finish",
    )(sums, basis, krylov)


def solution(mesh):
    placed = (
        P(None, None, "stream", None, "span"),
        P(),
        P(),
        P("stream", None, "span"),
        P("stream", None, "span"),
        P("stream", None, "span"),
    )
    return jax.shard_map(
        functools.partial(on_device, mesh.shape["stream"], mesh.shape["span"]),
        mesh=mesh,
        in_specs=placed,
        out_specs=(P(), P(), P(None, None, "stream", None, "span")),
        check_vma=False,
    )
```

```python
import functools

import jax
import jax.numpy as jnp
from jax import lax
from jax.experimental import pallas as pl
from jax.experimental.pallas import tpu as pltpu
from jax.sharding import PartitionSpec as P

STEPS = 4
DEEP = 4
WIDE = 2 * DEEP
MESH = pl.DeviceIdType.MESH


def total(terms):
    terms = list(terms)
    while len(terms) > 1:
        pairs = [terms[i] + terms[i + 1] for i in range(0, len(terms) - 1, 2)]
        terms = pairs + terms[len(terms) - len(terms) % 2 :]
    return terms[0]


def span_offsets(span):
    return () if span == 1 else ((1,) if span == 2 else (-1, 1))


def partners(span):
    dzs = span_offsets(span)
    return [(dx, 0) for dx in (-1, 1)] + [(0, dz) for dz in dzs] + [
        (dx, dz) for dx in (-1, 1) for dz in dzs
    ]


def near_and_far(streams):
    near = 16 if streams % 16 == 0 else 1
    return near, streams // near


def krylov_kernel(
    streams, spans,
    coeffs_in, mix_in, basis, base, span_speed, gain,
    krylov_out, sums_out,
    ext, states, held, pack, packs, edge, edges_in, strips, rim_rows, coef, strip_coef, acc, rows, near_rows, far_rows, coeffs, mix,
    in_sem, out_sem, send_sem, recv_sem, plane_send, plane_recv, row_send, row_recv,
):
    m, fields, planes = basis.shape[0], basis.shape[1], basis.shape[2]
    steps = STEPS
    lanes = basis.shape[4]
    sx, sz = lax.axis_index("stream"), lax.axis_index("span")
    near, far = near_and_far(streams)
    near_group = near * spans
    place = lax.rem(sx, near)
    near_index, far_index = place * spans + sz, sx // near

    def near_device(d):
        other = lax.rem(near_index + d, near_group)
        return (sx - place + other // spans, lax.rem(other, spans))

    def far_device(d):
        return (lax.rem(far_index + d, far) * near + place, sz)

    def device(dx, dz):
        return (lax.rem(sx + dx + streams, streams), lax.rem(sz + dz + spans, spans))

    barrier = pltpu.get_barrier_semaphore()

    own = pl.ds(DEEP, planes)
    loads = [
        pltpu.make_async_copy(basis.at[j], held.at[j], in_sem.at[j]) for j in range(m)
    ] + [
        pltpu.make_async_copy(ref, ext.at[fields + i, own], in_sem.at[m + i])
        for i, ref in enumerate((base, span_speed, gain))
    ] + [
        pltpu.make_async_copy(coeffs_in, coeffs, in_sem.at[m + 3]),
        pltpu.make_async_copy(mix_in, mix, in_sem.at[m + 4]),
    ]
    for load in loads:
        load.start()
    slots = partners(spans)
    greeted = [near_device(d) for d in range(1, near_group)]
    greeted += [far_device(d) for d in range(1, far)]
    if far > 1:
        greeted += [device(dx, dz) for dx, dz in slots]
    for other in greeted:
        pl.semaphore_signal(barrier, inc=1, device_id=other, device_id_type=MESH)

    lane = lax.broadcasted_iota(jnp.int32, (8, lanes), 1)
    row = lax.broadcasted_iota(jnp.int32, (8, lanes), 0)

    def packed(field, values):
        out = jnp.zeros((8, lanes), jnp.float32)
        for x in range(planes):
            at = WIDE * (x + DEEP)
            moved = pltpu.roll(values[x], DEEP + at, 1)
            out = jnp.where((lane >= at) & (lane < at + WIDE), moved, out)
        pack[field] = out

    sends, plane_sends = [], []

    def send(src, dst, dx, dz):
        i = len(sends)
        copy = pltpu.make_async_remote_copy(
            src_ref=src, dst_ref=dst, send_sem=send_sem.at[i], recv_sem=recv_sem.at[i],
            device_id=device(dx, dz), device_id_type=MESH,
        )
        copy.start()
        sends.append(copy)
        return copy

    for load in loads[m:]:
        load.wait()
    pl.semaphore_wait(barrier, len(greeted))
    third = pl.ds(fields, 3)
    send(ext.at[third, pl.ds(planes + 1, DEEP - 1)], ext.at[third, pl.ds(1, DEEP - 1)], 1, 0)
    send(ext.at[third, pl.ds(DEEP, DEEP - 1)], ext.at[third, pl.ds(planes + DEEP, DEEP - 1)], -1, 0)
    for i in range(3):
        packed(fields + i, [ext[fields + i, DEEP + x] for x in range(planes)])
    for load in loads[:m]:
        load.wait()
    weights = [coeffs[j] for j in range(m)]

    def start_field(f, carry):
        values = [total(weights[j] * held[j, f, x] for j in range(m)) for x in range(planes)]
        for x in range(planes):
            ext[f, DEEP + x] = values[x]
        packed(f, values)
        return carry

    for f in range(fields):
        start_field(f, 0)

    half = DEEP * WIDE
    per = lanes // half
    tops = planes * WIDE
    for e, begin in enumerate((half, tops)):
        for t in range(edge.shape[1]):
            out = jnp.zeros((8, lanes), jnp.float32)
            for j in range(per):
                f = t * per + j
                if f < fields + 3:
                    moved = pltpu.roll(pack[f], (j * half - begin) % lanes, 1)
                    out = jnp.where((lane >= j * half) & (lane < (j + 1) * half), moved, out)
            edge[e, t] = out
    for i, (dx, dz) in enumerate(slots):
        if dx == 0:
            send(pack, packs.at[i - 2], -dx, -dz)
    corner = [slot for slot in slots if slot[0] != 0]
    for i, (dx, dz) in enumerate(corner):
        send(edge.at[1 if dx == -1 else 0], edges_in.at[i], -dx, -dz)
    main = pl.ds(0, fields)
    for side, (src, dst) in enumerate(((planes, 0), (DEEP, planes + DEEP))):
        copy = pltpu.make_async_remote_copy(
            src_ref=ext.at[main, pl.ds(src, DEEP)], dst_ref=ext.at[main, pl.ds(dst, DEEP)],
            send_sem=plane_send.at[side], recv_sem=plane_recv.at[side],
            device_id=device(1 - 2 * side, 0), device_id_type=MESH,
        )
        copy.start()
        plane_sends.append(copy)

    upper = [(i, j) for i in range(m) for j in range(i, m)]
    krylov_pairs = [(k, l) for k in range(steps) for l in range(k, steps)]
    zero = jnp.zeros((8, lanes), jnp.float32)

    def basis_products(f, sums):
        for x in range(planes):
            b = [held[j, f, x] for j in range(m)]
            sums = [s + b[i] * b[j] for s, (i, j) in zip(sums, upper)]
        return sums

    basis_sums = lax.fori_loop(0, fields, basis_products, [zero] * len(upper))
    first = m * steps + len(krylov_pairs)
    for i, s in enumerate(basis_sums):
        acc[first + i] = s

    for copy in sends:
        copy.wait_recv()

    def cooked(u, w):
        return (
            0.05 - 0.5 * u, 0.05 + 0.5 * u, 0.05 - 0.5 * w, 0.05 + 0.5 * w
        )

    for x in range(1, planes + 2 * DEEP - 1):
        for i, value in enumerate(cooked(ext[fields, x], ext[fields + 1, x])):
            coef[i, x] = value

    inside = (lane >= half) & (lane < half + planes * WIDE)
    left_part = lane % WIDE < DEEP

    def strip_pair(f):
        tile, spot = f // per, f % per

        def whole(dz):
            here = pack[f] if dz == 0 else packs[slots.index((0, dz)) - 2, f]
            before = edges_in[corner.index((-1, dz)), tile]
            after = edges_in[corner.index((1, dz)), tile]
            before = pltpu.roll(before, (-spot * half) % lanes, 1)
            after = pltpu.roll(after, (tops + half - spot * half) % lanes, 1)
            return jnp.where(inside, here, jnp.where(lane < half, before, after))

        mine = whole(0)
        dzs = span_offsets(spans)
        left = whole(dzs[0]) if dzs else mine
        right = left if len(dzs) < 2 else whole(dzs[1])
        return jnp.where(left_part, left, mine), jnp.where(left_part, mine, right)

    for f in range(fields):
        for s, value in enumerate(strip_pair(f)):
            strips[0][f, s] = value
    us, ws, gs = (strip_pair(fields + i) for i in range(3))
    for s in range(2):
        for i, value in enumerate(cooked(us[s], ws[s]) + (gs[s],)):
            strip_coef[i, s] = value

    def walls(v):
        up = jnp.where(row < 7, pltpu.roll(v, 7, 0), 0.0)
        down = jnp.where(row > 0, pltpu.roll(v, 1, 0), 0.0)
        return up + down

    def read(k, f, x):
        return ext[f, x] if k == 0 else states[k - 1][f, x]

    def strip_step(k):
        def field(f, carry):
            weight = [mix[f, g] for g in range(fields)]
            done = []
            for s in range(2):
                mixed = total(a * strips[k][g, s] for g, a in enumerate(weight))
                v = strips[k][f, s]
                done.append(
                    strip_coef[0, s] * pltpu.roll(v, lanes - WIDE, 1)
                    + strip_coef[1, s] * pltpu.roll(v, WIDE, 1)
                    + strip_coef[2, s] * pltpu.roll(v, lanes - 1, 1)
                    + strip_coef[3, s] * pltpu.roll(v, 1, 1)
                    + (0.05 * walls(v) - 0.3 * v)
                    + strip_coef[4, s] * mixed
                )
            for s in range(2):
                strips[k + 1][f, s] = done[s]
            return carry

        for f in range(fields):
            field(f, 0)

    def rims(k):
        def field(f, carry):
            rim_rows[k][f] = jnp.where(
                lane % WIDE == DEEP - 1, strips[k][f, 0],
                pltpu.roll(strips[k][f, 1], lanes - 2, 1),
            )
            return carry

        for f in range(fields):
            field(f, 0)

    def advance(k, which, group):
        if not which:
            return

        def field_group(h, carry):
            some = [group * h + i for i in range(group)]
            weights = [[mix[f, g] for g in range(fields)] for f in some]
            sides = [rim_rows[k][f] for f in some]
            for x in which:
                vs = [read(k, g, x) for g in range(fields)]
                c0, c1, c2, c3 = (coef[i, x] for i in range(4))
                gain_here = ext[fields + 2, x]
                for f, weight, side in zip(some, weights, sides):
                    mixed = total(a * v for a, v in zip(weight, vs))
                    v = read(k, f, x)
                    rim = pltpu.roll(side, (2 * lanes - (WIDE * x + DEEP - 1)) % lanes, 1)
                    ahead = jnp.where(lane == lanes - 1, rim, pltpu.roll(v, lanes - 1, 1))
                    behind = jnp.where(lane == 0, rim, pltpu.roll(v, 1, 1))
                    states[k][f, x] = (
                        (c0 * read(k, f, x + 1) + c1 * read(k, f, x - 1))
                        + (c2 * ahead + c3 * behind)
                        + (0.05 * walls(v) - 0.3 * v)
                        + gain_here * mixed
                    )
            return carry

        for h in range(fields // group):
            field_group(h, 0)

    for k in range(steps):
        rims(k)
        if k < steps - 1:
            strip_step(k)
    large = 5 if fields % 5 == 0 else 1
    last = DEEP + planes
    early = [range(DEEP + 1 + k, last - 1 - k) for k in range(steps)]
    for k in range(steps):
        advance(k, early[k], large)
    for copy in plane_sends:
        copy.wait_recv()
    writes = []
    for k in range(steps):
        needed = range(1 + k, planes + 2 * DEEP - 1 - k)
        advance(k, [x for x in needed if x not in early[k]], large)
        write = pltpu.make_async_copy(states[k].at[:, own], krylov_out.at[k], out_sem.at[k])
        write.start()
        writes.append(write)

    def new_products(f, sums):
        for x in range(planes):
            b = [held[j, f, x] for j in range(m)]
            v = [states[k][f, DEEP + x] for k in range(steps)]
            terms = [b[j] * v[k] for j in range(m) for k in range(steps)]
            terms += [v[k] * v[l] for k, l in krylov_pairs]
            sums = [s + t for s, t in zip(sums, terms)]
        return sums

    new_sums = lax.fori_loop(0, fields, new_products, [zero] * first)
    count = first + len(upper)
    for i, s in enumerate(new_sums):
        rows[pl.ds(i, 1)] = jnp.sum(s, axis=0, keepdims=True)
    for i in range(first, count):
        rows[pl.ds(i, 1)] = jnp.sum(acc[i], axis=0, keepdims=True)
    for i in range(count, rows.shape[0]):
        rows[pl.ds(i, 1)] = jnp.zeros((1, lanes), jnp.float32)
    sums = jnp.sum(rows[...], axis=1, keepdims=True)
    at = lax.broadcasted_iota(jnp.int32, rows.shape, 0)
    spot = lax.broadcasted_iota(jnp.int32, rows.shape, 1)
    local = jnp.sum(jnp.where(at == spot, sums, 0.0), axis=0, keepdims=True)

    def summed(value, gathered, index, size, other, i):
        if size == 1:
            return value
        gathered[index] = value
        for d in range(1, size):
            pltpu.make_async_remote_copy(
                src_ref=gathered.at[index], dst_ref=gathered.at[index],
                send_sem=row_send.at[i], recv_sem=row_recv.at[i],
                device_id=other(d), device_id_type=MESH,
            ).start()
        others = gathered.at[pl.ds(0, size - 1)]
        everyone = pltpu.make_async_remote_copy(
            src_ref=others, dst_ref=others, send_sem=row_send.at[i], recv_sem=row_recv.at[i],
            device_id=other(1), device_id_type=MESH,
        )
        everyone.wait_recv()
        rows_sent.append(everyone)
        return jnp.sum(gathered[...], axis=0)

    rows_sent = []
    close = summed(local, near_rows, near_index, near_group, near_device, 0)
    sums_out[...] = summed(close, far_rows, far_index, far, far_device, 1)
    for copy in rows_sent:
        copy.wait_send()
    for copy in sends + plane_sends:
        copy.wait_send()
    for write in writes:
        write.wait()


def finish_kernel(
    ntot, chunks,
    sums, basis, krylov,
    proj_out, rfactor_out, new_out,
    result, out_sem,
):
    m, fields, planes = basis.shape[0], basis.shape[1], basis.shape[2]
    steps = krylov.shape[0]
    part = fields // chunks

    def piece(c):
        return pl.ds(c * part, part)

    shape = (8, basis.shape[4])
    row = sums[...] * (1.0 / ntot)

    def value(i):
        return jnp.broadcast_to(row[:, i : i + 1], shape)

    p = [[value(steps * j + k) for k in range(steps)] for j in range(m)]
    at = m * steps
    kk, bb = {}, {}
    for k in range(steps):
        for l in range(k, steps):
            kk[k, l] = value(at)
            at += 1
    for i in range(m):
        for j in range(i, m):
            bb[i, j] = bb[j, i] = value(at)
            at += 1
    q = [
        [2.0 * p[i][l] - total(bb[i, j] * p[j][l] for j in range(m)) for l in range(steps)]
        for i in range(m)
    ]
    low, inverse = {}, []
    for l in range(steps):
        for k in range(l, steps):
            g = kk[l, k] - total(p[i][l] * q[i][k] for i in range(m))
            for j in range(l):
                g = g - low[k, j] * low[l, j]
            if k == l:
                low[l, l] = jnp.sqrt(g)
                inverse.append(1.0 / low[l, l])
            else:
                low[k, l] = g * inverse[l]

    x = lax.broadcasted_iota(jnp.int32, shape, 0)
    y = lax.broadcasted_iota(jnp.int32, shape, 1)
    proj = jnp.zeros(shape, jnp.float32)
    for j in range(m):
        for k in range(steps):
            proj = jnp.where((x == j) & (y == k), p[j][k], proj)
    proj_out[...] = proj[:m, :steps]
    factor = jnp.zeros(shape, jnp.float32)
    for k, l in low:
        factor = jnp.where((x == l) & (y == k), low[k, l], factor)
    rfactor_out[...] = factor[:steps, :steps]

    writes = []
    for c in range(chunks):
        def one(i, carry, c=c):
            f = c * part + i
            for half in range(0, planes, 4):
                values = []
                for s in range(half, min(half + 4, planes)):
                    b = [basis[j, f, s] for j in range(m)]
                    done = []
                    for k in range(steps):
                        v = krylov[k, f, s] - total(p[j][k] * b[j] for j in range(m))
                        for l in range(k):
                            v = v - low[k, l] * done[l]
                        done.append(v * inverse[k])
                        values.append((k, s, done[k]))
                for k, s, value in values:
                    result[k, f, s] = value
            return carry

        lax.fori_loop(0, part, one, 0)
        write = pltpu.make_async_copy(
            result.at[:, piece(c)], new_out.at[:, piece(c)], out_sem.at[c]
        )
        write.start()
        writes.append(write)
    for write in writes:
        write.wait()


def on_device(streams, spans, basis, coeffs, mixing_matrix, base_speed, span_speed, polymer_gain):
    m, fields, planes, height, lanes = basis.shape
    n = streams * spans
    near, far = near_and_far(streams)
    f32 = jnp.float32
    deep = planes + 2 * DEEP
    count = m * STEPS + STEPS * (STEPS + 1) // 2 + m * (m + 1) // 2
    padded = -(-count // 8) * 8
    links = 2 + len(partners(spans))
    spans_beside = len(span_offsets(spans))
    corners = 2 + 2 * spans_beside
    tiles = -(-(fields + 3) * DEEP * WIDE // lanes)
    hbm = pl.BlockSpec(memory_space=pltpu.HBM)
    anywhere = pl.BlockSpec(memory_space=pl.ANY)
    vmem = pl.BlockSpec(memory_space=pltpu.VMEM)
    vector = (fields, planes, height, lanes)
    krylov, sums = pl.pallas_call(
        functools.partial(krylov_kernel, streams, spans),
        out_shape=(
            jax.ShapeDtypeStruct((STEPS,) + vector, f32),
            jax.ShapeDtypeStruct((1, lanes), f32),
        ),
        in_specs=[hbm] * 6,
        out_specs=(anywhere, vmem),
        scratch_shapes=[
            pltpu.VMEM((fields + 3, deep, height, lanes), f32),
            [pltpu.VMEM((fields, deep, height, lanes), f32)] * STEPS,
            pltpu.VMEM((m,) + vector, f32),
            pltpu.VMEM((fields + 3, height, lanes), f32),
            pltpu.VMEM((max(spans_beside, 1), fields + 3, height, lanes), f32),
            pltpu.VMEM((2, tiles, height, lanes), f32),
            pltpu.VMEM((corners, tiles, height, lanes), f32),
            [pltpu.VMEM((fields, 2, height, lanes), f32)] * STEPS,
            [pltpu.VMEM((fields, height, lanes), f32)] * STEPS,
            pltpu.VMEM((4, deep, height, lanes), f32),
            pltpu.VMEM((5, 2, height, lanes), f32),
            pltpu.VMEM((count, height, lanes), f32),
            pltpu.VMEM((padded, lanes), f32),
            pltpu.VMEM((near * spans, 1, lanes), f32),
            pltpu.VMEM((far, 1, lanes), f32),
            pltpu.SMEM(coeffs.shape, f32),
            pltpu.SMEM(mixing_matrix.shape, f32),
            pltpu.SemaphoreType.DMA((m + 5,)),
            pltpu.SemaphoreType.DMA((STEPS,)),
            pltpu.SemaphoreType.DMA((links,)),
            pltpu.SemaphoreType.DMA((links,)),
            pltpu.SemaphoreType.DMA((2,)),
            pltpu.SemaphoreType.DMA((2,)),
            pltpu.SemaphoreType.DMA((2,)),
            pltpu.SemaphoreType.DMA((2,)),
        ],
        compiler_params=pltpu.CompilerParams(
            collective_id=0, has_side_effects=True, vmem_limit_bytes=24 * 2**20
        ),
        name="krylov",
    )(*(
        pltpu.with_memory_space_constraint(x, pltpu.HBM)
        for x in (coeffs, mixing_matrix, basis, base_speed, span_speed, polymer_gain)
    ))
    chunks = 5 if fields % 5 == 0 else 1
    return pl.pallas_call(
        functools.partial(finish_kernel, float(m and basis[0].size * n), chunks),
        out_shape=(
            jax.ShapeDtypeStruct((m, STEPS), f32),
            jax.ShapeDtypeStruct((STEPS, STEPS), f32),
            jax.ShapeDtypeStruct((STEPS,) + vector, f32),
        ),
        in_specs=[vmem, vmem, vmem],
        out_specs=(vmem, vmem, hbm),
        scratch_shapes=[
            pltpu.VMEM((STEPS,) + vector, f32),
            pltpu.SemaphoreType.DMA((chunks,)),
        ],
        compiler_params=pltpu.CompilerParams(vmem_limit_bytes=24 * 2**20),
        name="finish",
    )(sums, basis, krylov)


def solution(mesh):
    placed = (
        P(None, None, "stream", None, "span"),
        P(),
        P(),
        P("stream", None, "span"),
        P("stream", None, "span"),
        P("stream", None, "span"),
    )
    return jax.shard_map(
        functools.partial(on_device, mesh.shape["stream"], mesh.shape["span"]),
        mesh=mesh,
        in_specs=placed,
        out_specs=(P(), P(), P(None, None, "stream", None, "span")),
        check_vma=False,
    )
```

```python
import functools

import jax
import jax.numpy as jnp
from jax import lax
from jax.experimental import pallas as pl
from jax.experimental.pallas import tpu as pltpu
from jax.sharding import PartitionSpec as P

STEPS = 4
DEEP = 4
WIDE = 2 * DEEP
MESH = pl.DeviceIdType.MESH


def total(terms):
    terms = list(terms)
    while len(terms) > 1:
        pairs = [terms[i] + terms[i + 1] for i in range(0, len(terms) - 1, 2)]
        terms = pairs + terms[len(terms) - len(terms) % 2 :]
    return terms[0]


def span_offsets(span):
    return () if span == 1 else ((1,) if span == 2 else (-1, 1))


def partners(span):
    dzs = span_offsets(span)
    return [(dx, 0) for dx in (-1, 1)] + [(0, dz) for dz in dzs] + [
        (dx, dz) for dx in (-1, 1) for dz in dzs
    ]


def near_and_far(streams):
    near = 16 if streams % 16 == 0 else 1
    return near, streams // near


def krylov_kernel(
    streams, spans,
    coeffs_in, mix_in, basis, base, span_speed, gain,
    krylov_out, sums_out,
    ext, states, held, pack, packs, edge, edges_in, strips, rim_rows, coef, strip_coef, rows, near_rows, far_rows, coeffs, mix,
    in_sem, out_sem, send_sem, recv_sem, plane_send, plane_recv, row_send, row_recv,
):
    m, fields, planes = basis.shape[0], basis.shape[1], basis.shape[2]
    steps = STEPS
    lanes = basis.shape[4]
    sx, sz = lax.axis_index("stream"), lax.axis_index("span")
    near, far = near_and_far(streams)
    near_group = near * spans
    place = lax.rem(sx, near)
    near_index, far_index = place * spans + sz, sx // near

    def turned(value, size):
        return jnp.where(value >= size, value - size, value)

    near_streams = [sx - place + turned(place + d, near) for d in range(near)]
    near_spans = [turned(sz + d, spans) for d in range(spans)]

    def near_device(d):
        return (near_streams[d // spans], near_spans[d % spans])

    def far_device(d):
        return (lax.rem(far_index + d, far) * near + place, sz)

    def device(dx, dz):
        return (lax.rem(sx + dx + streams, streams), lax.rem(sz + dz + spans, spans))

    barrier = pltpu.get_barrier_semaphore()

    own = pl.ds(DEEP, planes)
    part = fields // 5 if fields % 5 == 0 else fields
    pieces = [pl.ds(f, part) for f in range(0, fields, part)]
    loads = [
        pltpu.make_async_copy(basis.at[:, piece], held.at[:, piece], in_sem.at[5 + c])
        for c, piece in enumerate(pieces)
    ] + [
        pltpu.make_async_copy(ref, ext.at[fields + i, own], in_sem.at[i])
        for i, ref in enumerate((base, span_speed, gain))
    ] + [
        pltpu.make_async_copy(coeffs_in, coeffs, in_sem.at[3]),
        pltpu.make_async_copy(mix_in, mix, in_sem.at[4]),
    ]
    for load in loads[len(pieces):] + loads[: len(pieces)]:
        load.start()
    slots = partners(spans)
    greeted = [near_device(d) for d in range(1, near_group)]
    greeted += [far_device(d) for d in range(1, far)]
    if far > 1:
        greeted += [device(dx, dz) for dx, dz in slots]
    for other in greeted:
        pl.semaphore_signal(barrier, inc=1, device_id=other, device_id_type=MESH)

    lane = lax.broadcasted_iota(jnp.int32, (8, lanes), 1)
    row = lax.broadcasted_iota(jnp.int32, (8, lanes), 0)

    def packed(field, values):
        out = jnp.zeros((8, lanes), jnp.float32)
        for x in range(planes):
            at = WIDE * (x + DEEP)
            moved = pltpu.roll(values[x], DEEP + at, 1)
            out = jnp.where((lane >= at) & (lane < at + WIDE), moved, out)
        pack[field] = out

    sends, plane_sends = [], []

    def send(src, dst, dx, dz):
        i = len(sends)
        copy = pltpu.make_async_remote_copy(
            src_ref=src, dst_ref=dst, send_sem=send_sem.at[i], recv_sem=recv_sem.at[i],
            device_id=device(dx, dz), device_id_type=MESH,
        )
        copy.start()
        sends.append(copy)
        return copy

    for load in loads[len(pieces):]:
        load.wait()
    pl.semaphore_wait(barrier, len(greeted))
    third = pl.ds(fields, 3)
    send(ext.at[third, pl.ds(planes + 1, DEEP - 1)], ext.at[third, pl.ds(1, DEEP - 1)], 1, 0)
    send(ext.at[third, pl.ds(DEEP, DEEP - 1)], ext.at[third, pl.ds(planes + DEEP, DEEP - 1)], -1, 0)
    for i in range(3):
        packed(fields + i, [ext[fields + i, DEEP + x] for x in range(planes)])
    weights = [coeffs[j] for j in range(m)]

    def start_field(f, carry):
        values = [total(weights[j] * held[j, f, x] for j in range(m)) for x in range(planes)]
        for x in range(planes):
            ext[f, DEEP + x] = values[x]
        packed(f, values)
        return carry

    for f in range(fields):
        if f % part == 0:
            loads[f // part].wait()
        start_field(f, 0)

    half = DEEP * WIDE
    per = lanes // half
    tops = planes * WIDE
    for e, begin in enumerate((half, tops)):
        for t in range(edge.shape[1]):
            out = jnp.zeros((8, lanes), jnp.float32)
            for j in range(per):
                f = t * per + j
                if f < fields + 3:
                    moved = pltpu.roll(pack[f], (j * half - begin) % lanes, 1)
                    out = jnp.where((lane >= j * half) & (lane < (j + 1) * half), moved, out)
            edge[e, t] = out
    for i, (dx, dz) in enumerate(slots):
        if dx == 0:
            send(pack, packs.at[i - 2], -dx, -dz)
    corner = [slot for slot in slots if slot[0] != 0]
    for i, (dx, dz) in enumerate(corner):
        send(edge.at[1 if dx == -1 else 0], edges_in.at[i], -dx, -dz)
    main = pl.ds(0, fields)
    for side, (src, dst) in enumerate(((planes, 0), (DEEP, planes + DEEP))):
        copy = pltpu.make_async_remote_copy(
            src_ref=ext.at[main, pl.ds(src, DEEP)], dst_ref=ext.at[main, pl.ds(dst, DEEP)],
            send_sem=plane_send.at[side], recv_sem=plane_recv.at[side],
            device_id=device(1 - 2 * side, 0), device_id_type=MESH,
        )
        copy.start()
        plane_sends.append(copy)

    upper = [(i, j) for i in range(m) for j in range(i, m)]
    krylov_pairs = [(k, l) for k in range(steps) for l in range(k, steps)]
    zero = jnp.zeros((8, lanes), jnp.float32)

    def basis_products(f, sums):
        for x in range(planes):
            b = [held[j, f, x] for j in range(m)]
            sums = [s + b[i] * b[j] for s, (i, j) in zip(sums, upper)]
        return sums

    basis_sums = lax.fori_loop(0, fields, basis_products, [zero] * len(upper))
    first = m * steps + len(krylov_pairs)
    count = first + len(upper)
    for i, s in enumerate(basis_sums):
        rows[pl.ds(first + i, 1)] = jnp.sum(s, axis=0, keepdims=True)
    for i in range(count, rows.shape[0]):
        rows[pl.ds(i, 1)] = jnp.zeros((1, lanes), jnp.float32)

    for copy in sends:
        copy.wait_recv()

    def cooked(u, w):
        return (
            0.05 - 0.5 * u, 0.05 + 0.5 * u, 0.05 - 0.5 * w, 0.05 + 0.5 * w
        )

    for x in range(1, planes + 2 * DEEP - 1):
        for i, value in enumerate(cooked(ext[fields, x], ext[fields + 1, x])):
            coef[i, x] = value

    inside = (lane >= half) & (lane < half + planes * WIDE)
    left_part = lane % WIDE < DEEP

    def strip_pair(f):
        tile, spot = f // per, f % per

        def whole(dz):
            here = pack[f] if dz == 0 else packs[slots.index((0, dz)) - 2, f]
            before = edges_in[corner.index((-1, dz)), tile]
            after = edges_in[corner.index((1, dz)), tile]
            before = pltpu.roll(before, (-spot * half) % lanes, 1)
            after = pltpu.roll(after, (tops + half - spot * half) % lanes, 1)
            return jnp.where(inside, here, jnp.where(lane < half, before, after))

        mine = whole(0)
        dzs = span_offsets(spans)
        left = whole(dzs[0]) if dzs else mine
        right = left if len(dzs) < 2 else whole(dzs[1])
        return jnp.where(left_part, left, mine), jnp.where(left_part, mine, right)

    for f in range(fields):
        for s, value in enumerate(strip_pair(f)):
            strips[0][f, s] = value
    us, ws, gs = (strip_pair(fields + i) for i in range(3))
    for s in range(2):
        for i, value in enumerate(cooked(us[s], ws[s]) + (gs[s],)):
            strip_coef[i, s] = value

    above = jnp.where(row < 7, 0.05, 0.0)
    below = jnp.where(row > 0, 0.05, 0.0)

    def walls(v):
        return above * pltpu.roll(v, 7, 0) + below * pltpu.roll(v, 1, 0)

    def read(k, f, x):
        return ext[f, x] if k == 0 else states[k - 1][f, x]

    def strip_step(k):
        def field(f, carry):
            weight = [mix[f, g] for g in range(fields)]
            done = []
            for s in range(2):
                mixed = total(a * strips[k][g, s] for g, a in enumerate(weight))
                v = strips[k][f, s]
                done.append(
                    strip_coef[0, s] * pltpu.roll(v, lanes - WIDE, 1)
                    + strip_coef[1, s] * pltpu.roll(v, WIDE, 1)
                    + strip_coef[2, s] * pltpu.roll(v, lanes - 1, 1)
                    + strip_coef[3, s] * pltpu.roll(v, 1, 1)
                    + (walls(v) - 0.3 * v)
                    + strip_coef[4, s] * mixed
                )
            for s in range(2):
                strips[k + 1][f, s] = done[s]
            return carry

        for f in range(fields):
            field(f, 0)

    def rims(k):
        def field(f, carry):
            rim_rows[k][f] = jnp.where(
                lane % WIDE == DEEP - 1, strips[k][f, 0],
                pltpu.roll(strips[k][f, 1], lanes - 2, 1),
            )
            return carry

        for f in range(fields):
            field(f, 0)

    def advance(k, which, group):
        if not which:
            return

        def field_group(h, carry):
            some = [group * h + i for i in range(group)]
            weights = [[mix[f, g] for g in range(fields)] for f in some]
            sides = [rim_rows[k][f] for f in some]
            for x in which:
                vs = [read(k, g, x) for g in range(fields)]
                c0, c1, c2, c3 = (coef[i, x] for i in range(4))
                gain_here = ext[fields + 2, x]
                for f, weight, side in zip(some, weights, sides):
                    mixed = total(a * v for a, v in zip(weight, vs))
                    v = read(k, f, x)
                    rim = pltpu.roll(side, (2 * lanes - (WIDE * x + DEEP - 1)) % lanes, 1)
                    ahead = jnp.where(lane == lanes - 1, rim, pltpu.roll(v, lanes - 1, 1))
                    behind = jnp.where(lane == 0, rim, pltpu.roll(v, 1, 1))
                    states[k][f, x] = (
                        (c0 * read(k, f, x + 1) + c1 * read(k, f, x - 1))
                        + (c2 * ahead + c3 * behind)
                        + (walls(v) - 0.3 * v)
                        + gain_here * mixed
                    )
            return carry

        for h in range(fields // group):
            field_group(h, 0)

    for k in range(steps):
        rims(k)
        if k < steps - 1:
            strip_step(k)
    large = 5 if fields % 5 == 0 else 1
    last = DEEP + planes
    early = [range(DEEP + 1 + k, last - 1 - k) for k in range(steps)]
    for k in range(steps):
        advance(k, early[k], large)
    for copy in plane_sends:
        copy.wait_recv()
    writes = []
    for k in range(steps):
        needed = range(1 + k, planes + 2 * DEEP - 1 - k)
        advance(k, [x for x in needed if x not in early[k]], large)
        write = pltpu.make_async_copy(states[k].at[:, own], krylov_out.at[k], out_sem.at[k])
        write.start()
        writes.append(write)

    def new_products(f, sums):
        for x in range(planes):
            b = [held[j, f, x] for j in range(m)]
            v = [states[k][f, DEEP + x] for k in range(steps)]
            terms = [b[j] * v[k] for j in range(m) for k in range(steps)]
            terms += [v[k] * v[l] for k, l in krylov_pairs]
            sums = [s + t for s, t in zip(sums, terms)]
        return sums

    new_sums = [zero] * first
    for f in range(fields):
        new_sums = new_products(f, new_sums)
    for i, s in enumerate(new_sums):
        rows[pl.ds(i, 1)] = jnp.sum(s, axis=0, keepdims=True)
    sums = jnp.sum(rows[...], axis=1, keepdims=True)
    at = lax.broadcasted_iota(jnp.int32, rows.shape, 0)
    spot = lax.broadcasted_iota(jnp.int32, rows.shape, 1)
    local = jnp.sum(jnp.where(at == spot, sums, 0.0), axis=0, keepdims=True)

    def summed(value, gathered, index, size, other, i):
        if size == 1:
            return value
        gathered[index] = value
        for d in range(1, size):
            pltpu.make_async_remote_copy(
                src_ref=gathered.at[index], dst_ref=gathered.at[index],
                send_sem=row_send.at[i], recv_sem=row_recv.at[i],
                device_id=other(d), device_id_type=MESH,
            ).start()
        others = gathered.at[pl.ds(0, size - 1)]
        everyone = pltpu.make_async_remote_copy(
            src_ref=others, dst_ref=others, send_sem=row_send.at[i], recv_sem=row_recv.at[i],
            device_id=other(1), device_id_type=MESH,
        )
        everyone.wait_recv()
        rows_sent.append(everyone)
        return jnp.sum(gathered[...], axis=0)

    rows_sent = []
    close = summed(local, near_rows, near_index, near_group, near_device, 0)
    sums_out[...] = summed(close, far_rows, far_index, far, far_device, 1)
    for copy in rows_sent:
        copy.wait_send()
    for copy in sends + plane_sends:
        copy.wait_send()
    for write in writes:
        write.wait()


def finish_kernel(
    ntot, chunks,
    sums, basis, krylov,
    proj_out, rfactor_out, new_out,
    result, out_sem,
):
    m, fields, planes = basis.shape[0], basis.shape[1], basis.shape[2]
    steps = krylov.shape[0]
    part = fields // chunks

    def piece(c):
        return pl.ds(c * part, part)

    shape = (8, basis.shape[4])
    row = sums[...] * (1.0 / ntot)

    def value(i):
        return jnp.broadcast_to(row[:, i : i + 1], shape)

    p = [[value(steps * j + k) for k in range(steps)] for j in range(m)]
    at = m * steps
    kk, bb = {}, {}
    for k in range(steps):
        for l in range(k, steps):
            kk[k, l] = value(at)
            at += 1
    for i in range(m):
        for j in range(i, m):
            bb[i, j] = bb[j, i] = value(at)
            at += 1
    q = [
        [2.0 * p[i][l] - total(bb[i, j] * p[j][l] for j in range(m)) for l in range(steps)]
        for i in range(m)
    ]
    low, inverse = {}, []
    for l in range(steps):
        for k in range(l, steps):
            g = kk[l, k] - total(p[i][l] * q[i][k] for i in range(m))
            for j in range(l):
                g = g - low[k, j] * low[l, j]
            if k == l:
                low[l, l] = jnp.sqrt(g)
                inverse.append(1.0 / low[l, l])
            else:
                low[k, l] = g * inverse[l]

    x = lax.broadcasted_iota(jnp.int32, shape, 0)
    y = lax.broadcasted_iota(jnp.int32, shape, 1)
    proj = jnp.zeros(shape, jnp.float32)
    for j in range(m):
        for k in range(steps):
            proj = jnp.where((x == j) & (y == k), p[j][k], proj)
    proj_out[...] = proj[:m, :steps]
    factor = jnp.zeros(shape, jnp.float32)
    for k, l in low:
        factor = jnp.where((x == l) & (y == k), low[k, l], factor)
    rfactor_out[...] = factor[:steps, :steps]

    writes = []
    for c in range(chunks):
        def one(i, carry, c=c):
            f = c * part + i
            for half in range(0, planes, 4):
                values = []
                for s in range(half, min(half + 4, planes)):
                    b = [basis[j, f, s] for j in range(m)]
                    done = []
                    for k in range(steps):
                        v = krylov[k, f, s] - total(p[j][k] * b[j] for j in range(m))
                        for l in range(k):
                            v = v - low[k, l] * done[l]
                        done.append(v * inverse[k])
                        values.append((k, s, done[k]))
                for k, s, value in values:
                    result[k, f, s] = value
            return carry

        for i in range(part):
            one(i, 0)
        write = pltpu.make_async_copy(
            result.at[:, piece(c)], new_out.at[:, piece(c)], out_sem.at[c]
        )
        write.start()
        writes.append(write)
    for write in writes:
        write.wait()


def on_device(streams, spans, basis, coeffs, mixing_matrix, base_speed, span_speed, polymer_gain):
    m, fields, planes, height, lanes = basis.shape
    n = streams * spans
    near, far = near_and_far(streams)
    f32 = jnp.float32
    deep = planes + 2 * DEEP
    count = m * STEPS + STEPS * (STEPS + 1) // 2 + m * (m + 1) // 2
    padded = -(-count // 8) * 8
    links = 2 + len(partners(spans))
    spans_beside = len(span_offsets(spans))
    corners = 2 + 2 * spans_beside
    tiles = -(-(fields + 3) * DEEP * WIDE // lanes)
    hbm = pl.BlockSpec(memory_space=pltpu.HBM)
    anywhere = pl.BlockSpec(memory_space=pl.ANY)
    vmem = pl.BlockSpec(memory_space=pltpu.VMEM)
    vector = (fields, planes, height, lanes)
    krylov, sums = pl.pallas_call(
        functools.partial(krylov_kernel, streams, spans),
        out_shape=(
            jax.ShapeDtypeStruct((STEPS,) + vector, f32),
            jax.ShapeDtypeStruct((1, lanes), f32),
        ),
        in_specs=[hbm] * 6,
        out_specs=(anywhere, vmem),
        scratch_shapes=[
            pltpu.VMEM((fields + 3, deep, height, lanes), f32),
            [pltpu.VMEM((fields, deep, height, lanes), f32)] * STEPS,
            pltpu.VMEM((m,) + vector, f32),
            pltpu.VMEM((fields + 3, height, lanes), f32),
            pltpu.VMEM((max(spans_beside, 1), fields + 3, height, lanes), f32),
            pltpu.VMEM((2, tiles, height, lanes), f32),
            pltpu.VMEM((corners, tiles, height, lanes), f32),
            [pltpu.VMEM((fields, 2, height, lanes), f32)] * STEPS,
            [pltpu.VMEM((fields, height, lanes), f32)] * STEPS,
            pltpu.VMEM((4, deep, height, lanes), f32),
            pltpu.VMEM((5, 2, height, lanes), f32),
            pltpu.VMEM((padded, lanes), f32),
            pltpu.VMEM((near * spans, 1, lanes), f32),
            pltpu.VMEM((far, 1, lanes), f32),
            pltpu.SMEM(coeffs.shape, f32),
            pltpu.SMEM(mixing_matrix.shape, f32),
            pltpu.SemaphoreType.DMA((10,)),
            pltpu.SemaphoreType.DMA((STEPS,)),
            pltpu.SemaphoreType.DMA((links,)),
            pltpu.SemaphoreType.DMA((links,)),
            pltpu.SemaphoreType.DMA((2,)),
            pltpu.SemaphoreType.DMA((2,)),
            pltpu.SemaphoreType.DMA((2,)),
            pltpu.SemaphoreType.DMA((2,)),
        ],
        compiler_params=pltpu.CompilerParams(
            collective_id=0, has_side_effects=True, vmem_limit_bytes=24 * 2**20
        ),
        name="krylov",
    )(*(
        pltpu.with_memory_space_constraint(x, pltpu.HBM)
        for x in (coeffs, mixing_matrix, basis, base_speed, span_speed, polymer_gain)
    ))
    chunks = 5 if fields % 5 == 0 else 1
    return pl.pallas_call(
        functools.partial(finish_kernel, float(m and basis[0].size * n), chunks),
        out_shape=(
            jax.ShapeDtypeStruct((m, STEPS), f32),
            jax.ShapeDtypeStruct((STEPS, STEPS), f32),
            jax.ShapeDtypeStruct((STEPS,) + vector, f32),
        ),
        in_specs=[vmem, vmem, vmem],
        out_specs=(vmem, vmem, hbm),
        scratch_shapes=[
            pltpu.VMEM((STEPS,) + vector, f32),
            pltpu.SemaphoreType.DMA((chunks,)),
        ],
        compiler_params=pltpu.CompilerParams(vmem_limit_bytes=24 * 2**20),
        name="finish",
    )(sums, basis, krylov)


def solution(mesh):
    placed = (
        P(None, None, "stream", None, "span"),
        P(),
        P(),
        P("stream", None, "span"),
        P("stream", None, "span"),
        P("stream", None, "span"),
    )
    return jax.shard_map(
        functools.partial(on_device, mesh.shape["stream"], mesh.shape["span"]),
        mesh=mesh,
        in_specs=placed,
        out_specs=(P(), P(), P(None, None, "stream", None, "span")),
        check_vma=False,
    )
```

```python
import functools

import jax
import jax.numpy as jnp
from jax import lax
from jax.experimental import pallas as pl
from jax.experimental.pallas import tpu as pltpu
from jax.sharding import PartitionSpec as P

STEPS = 4
DEEP = 4
WIDE = 2 * DEEP
MESH = pl.DeviceIdType.MESH


def total(terms):
    terms = list(terms)
    while len(terms) > 1:
        pairs = [terms[i] + terms[i + 1] for i in range(0, len(terms) - 1, 2)]
        terms = pairs + terms[len(terms) - len(terms) % 2 :]
    return terms[0]


def span_offsets(span):
    return () if span == 1 else ((1,) if span == 2 else (-1, 1))


def partners(span):
    dzs = span_offsets(span)
    return [(dx, 0) for dx in (-1, 1)] + [(0, dz) for dz in dzs] + [
        (dx, dz) for dx in (-1, 1) for dz in dzs
    ]


def near_and_far(streams):
    near = 16 if streams % 16 == 0 else 1
    return near, streams // near


def krylov_kernel(
    streams, spans,
    coeffs_in, mix_in, basis, base, span_speed, gain,
    krylov_out, sums_out,
    ext, states, held, pack, packs, edge, edges_in, strips, rim_rows, coef, strip_coef, rows, near_rows, far_rows, coeffs, mix,
    in_sem, out_sem, send_sem, recv_sem, plane_send, plane_recv, row_send, row_recv,
):
    m, fields, planes = basis.shape[0], basis.shape[1], basis.shape[2]
    steps = STEPS
    lanes = basis.shape[4]
    sx, sz = lax.axis_index("stream"), lax.axis_index("span")
    near, far = near_and_far(streams)
    near_group = near * spans
    place = lax.rem(sx, near)
    near_index, far_index = place * spans + sz, sx // near

    def turned(value, size):
        return jnp.where(value >= size, value - size, value)

    near_streams = [sx - place + turned(place + d, near) for d in range(near)]
    near_spans = [turned(sz + d, spans) for d in range(spans)]

    def near_device(d):
        return (near_streams[d // spans], near_spans[d % spans])

    def far_device(d):
        return (lax.rem(far_index + d, far) * near + place, sz)

    def device(dx, dz):
        return (lax.rem(sx + dx + streams, streams), lax.rem(sz + dz + spans, spans))

    barrier = pltpu.get_barrier_semaphore()

    own = pl.ds(DEEP, planes)
    part = fields // 5 if fields % 5 == 0 else fields
    pieces = [pl.ds(f, part) for f in range(0, fields, part)]
    loads = [
        pltpu.make_async_copy(basis.at[:, piece], held.at[:, piece], in_sem.at[5 + c])
        for c, piece in enumerate(pieces)
    ] + [
        pltpu.make_async_copy(ref, ext.at[fields + i, own], in_sem.at[i])
        for i, ref in enumerate((base, span_speed, gain))
    ] + [
        pltpu.make_async_copy(coeffs_in, coeffs, in_sem.at[3]),
        pltpu.make_async_copy(mix_in, mix, in_sem.at[4]),
    ]
    for load in loads[len(pieces):] + loads[: len(pieces)]:
        load.start()
    slots = partners(spans)
    greeted = [near_device(d) for d in range(1, near_group)]
    greeted += [far_device(d) for d in range(1, far)]
    if far > 1:
        greeted += [device(dx, dz) for dx, dz in slots]
    for other in greeted:
        pl.semaphore_signal(barrier, inc=1, device_id=other, device_id_type=MESH)

    lane = lax.broadcasted_iota(jnp.int32, (8, lanes), 1)
    row = lax.broadcasted_iota(jnp.int32, (8, lanes), 0)

    def packed(field, values):
        out = jnp.zeros((8, lanes), jnp.float32)
        for x in range(planes):
            at = WIDE * (x + DEEP)
            moved = pltpu.roll(values[x], DEEP + at, 1)
            out = jnp.where((lane >= at) & (lane < at + WIDE), moved, out)
        pack[field] = out

    sends, plane_sends = [], []

    def send(src, dst, dx, dz):
        i = len(sends)
        copy = pltpu.make_async_remote_copy(
            src_ref=src, dst_ref=dst, send_sem=send_sem.at[i], recv_sem=recv_sem.at[i],
            device_id=device(dx, dz), device_id_type=MESH,
        )
        copy.start()
        sends.append(copy)
        return copy

    for load in loads[len(pieces):]:
        load.wait()
    pl.semaphore_wait(barrier, len(greeted))
    third = pl.ds(fields, 3)
    send(ext.at[third, pl.ds(planes + 1, DEEP - 1)], ext.at[third, pl.ds(1, DEEP - 1)], 1, 0)
    send(ext.at[third, pl.ds(DEEP, DEEP - 1)], ext.at[third, pl.ds(planes + DEEP, DEEP - 1)], -1, 0)
    for i in range(3):
        packed(fields + i, [ext[fields + i, DEEP + x] for x in range(planes)])
    weights = [coeffs[j] for j in range(m)]

    def start_field(f, carry):
        values = [total(weights[j] * held[j, f, x] for j in range(m)) for x in range(planes)]
        for x in range(planes):
            ext[f, DEEP + x] = values[x]
        packed(f, values)
        return carry

    for f in range(fields):
        if f % part == 0:
            loads[f // part].wait()
        start_field(f, 0)

    half = DEEP * WIDE
    per = lanes // half
    tops = planes * WIDE
    for e, begin in enumerate((half, tops)):
        for t in range(edge.shape[1]):
            out = jnp.zeros((8, lanes), jnp.float32)
            for j in range(per):
                f = t * per + j
                if f < fields + 3:
                    moved = pltpu.roll(pack[f], (j * half - begin) % lanes, 1)
                    out = jnp.where((lane >= j * half) & (lane < (j + 1) * half), moved, out)
            edge[e, t] = out
    for i, (dx, dz) in enumerate(slots):
        if dx == 0:
            send(pack, packs.at[i - 2], -dx, -dz)
    corner = [slot for slot in slots if slot[0] != 0]
    for i, (dx, dz) in enumerate(corner):
        send(edge.at[1 if dx == -1 else 0], edges_in.at[i], -dx, -dz)
    main = pl.ds(0, fields)
    mid = DEEP // 2
    for i, (src, dst, dx) in enumerate((
        (planes + mid, mid, 1), (DEEP, planes + DEEP, -1),
        (planes, 0, 1), (DEEP + mid, planes + DEEP + mid, -1),
    )):
        copy = pltpu.make_async_remote_copy(
            src_ref=ext.at[main, pl.ds(src, mid)], dst_ref=ext.at[main, pl.ds(dst, mid)],
            send_sem=plane_send.at[i], recv_sem=plane_recv.at[i],
            device_id=device(dx, 0), device_id_type=MESH,
        )
        copy.start()
        plane_sends.append(copy)

    upper = [(i, j) for i in range(m) for j in range(i, m)]
    krylov_pairs = [(k, l) for k in range(steps) for l in range(k, steps)]
    zero = jnp.zeros((8, lanes), jnp.float32)

    def basis_products(f, sums):
        for x in range(planes):
            b = [held[j, f, x] for j in range(m)]
            sums = [s + b[i] * b[j] for s, (i, j) in zip(sums, upper)]
        return sums

    basis_sums = lax.fori_loop(0, fields, basis_products, [zero] * len(upper))
    first = m * steps + len(krylov_pairs)
    count = first + len(upper)
    for i, s in enumerate(basis_sums):
        rows[pl.ds(first + i, 1)] = jnp.sum(s, axis=0, keepdims=True)
    for i in range(count, rows.shape[0]):
        rows[pl.ds(i, 1)] = jnp.zeros((1, lanes), jnp.float32)

    for copy in sends:
        copy.wait_recv()

    def cooked(u, w):
        return (
            0.05 - 0.5 * u, 0.05 + 0.5 * u, 0.05 - 0.5 * w, 0.05 + 0.5 * w
        )

    for x in range(1, planes + 2 * DEEP - 1):
        for i, value in enumerate(cooked(ext[fields, x], ext[fields + 1, x])):
            coef[i, x] = value

    inside = (lane >= half) & (lane < half + planes * WIDE)
    left_part = lane % WIDE < DEEP

    def strip_pair(f):
        tile, spot = f // per, f % per

        def whole(dz):
            here = pack[f] if dz == 0 else packs[slots.index((0, dz)) - 2, f]
            before = edges_in[corner.index((-1, dz)), tile]
            after = edges_in[corner.index((1, dz)), tile]
            before = pltpu.roll(before, (-spot * half) % lanes, 1)
            after = pltpu.roll(after, (tops + half - spot * half) % lanes, 1)
            return jnp.where(inside, here, jnp.where(lane < half, before, after))

        mine = whole(0)
        dzs = span_offsets(spans)
        left = whole(dzs[0]) if dzs else mine
        right = left if len(dzs) < 2 else whole(dzs[1])
        return jnp.where(left_part, left, mine), jnp.where(left_part, mine, right)

    for f in range(fields):
        for s, value in enumerate(strip_pair(f)):
            strips[0][f, s] = value
    us, ws, gs = (strip_pair(fields + i) for i in range(3))
    for s in range(2):
        for i, value in enumerate(cooked(us[s], ws[s]) + (gs[s],)):
            strip_coef[i, s] = value

    above = jnp.where(row < 7, 0.05, 0.0)
    below = jnp.where(row > 0, 0.05, 0.0)

    def walls(v):
        return above * pltpu.roll(v, 7, 0) + below * pltpu.roll(v, 1, 0)

    def read(k, f, x):
        return ext[f, x] if k == 0 else states[k - 1][f, x]

    def strip_step(k):
        def field(f, carry):
            weight = [mix[f, g] for g in range(fields)]
            done = []
            for s in range(2):
                mixed = total(a * strips[k][g, s] for g, a in enumerate(weight))
                v = strips[k][f, s]
                done.append(
                    strip_coef[0, s] * pltpu.roll(v, lanes - WIDE, 1)
                    + strip_coef[1, s] * pltpu.roll(v, WIDE, 1)
                    + strip_coef[2, s] * pltpu.roll(v, lanes - 1, 1)
                    + strip_coef[3, s] * pltpu.roll(v, 1, 1)
                    + (walls(v) - 0.3 * v)
                    + strip_coef[4, s] * mixed
                )
            for s in range(2):
                strips[k + 1][f, s] = done[s]
            return carry

        for f in range(fields):
            field(f, 0)

    def rims(k):
        def field(f, carry):
            rim_rows[k][f] = jnp.where(
                lane % WIDE == DEEP - 1, strips[k][f, 0],
                pltpu.roll(strips[k][f, 1], lanes - 2, 1),
            )
            return carry

        for f in range(fields):
            field(f, 0)

    def advance(k, which, group):
        if not which:
            return

        def field_group(h, carry):
            some = [group * h + i for i in range(group)]
            weights = [[mix[f, g] for g in range(fields)] for f in some]
            sides = [rim_rows[k][f] for f in some]
            for x in which:
                vs = [read(k, g, x) for g in range(fields)]
                c0, c1, c2, c3 = (coef[i, x] for i in range(4))
                gain_here = ext[fields + 2, x]
                for f, weight, side in zip(some, weights, sides):
                    mixed = total(a * v for a, v in zip(weight, vs))
                    v = read(k, f, x)
                    rim = pltpu.roll(side, (2 * lanes - (WIDE * x + DEEP - 1)) % lanes, 1)
                    ahead = jnp.where(lane == lanes - 1, rim, pltpu.roll(v, lanes - 1, 1))
                    behind = jnp.where(lane == 0, rim, pltpu.roll(v, 1, 1))
                    states[k][f, x] = (
                        (c0 * read(k, f, x + 1) + c1 * read(k, f, x - 1))
                        + (c2 * ahead + c3 * behind)
                        + (walls(v) - 0.3 * v)
                        + gain_here * mixed
                    )
            return carry

        for h in range(fields // group):
            field_group(h, 0)

    for k in range(steps):
        rims(k)
        if k < steps - 1:
            strip_step(k)
    large = 5 if fields % 5 == 0 else 1
    last = DEEP + planes
    ready = [range(DEEP + 1 + k, last - 1 - k) for k in range(steps)]
    for k in range(steps):
        advance(k, ready[k], large)
    for copy in plane_sends[:2]:
        copy.wait_recv()
    for k in range(steps):
        wider = range(DEEP + 1 + k - mid, last - 1 - k + mid)
        advance(k, [x for x in wider if x not in ready[k]], large)
        ready[k] = wider
    for copy in plane_sends[2:]:
        copy.wait_recv()
    writes = []
    for k in range(steps):
        needed = range(1 + k, planes + 2 * DEEP - 1 - k)
        advance(k, [x for x in needed if x not in ready[k]], large)
        write = pltpu.make_async_copy(states[k].at[:, own], krylov_out.at[k], out_sem.at[k])
        write.start()
        writes.append(write)

    def new_products(f, sums):
        for x in range(planes):
            b = [held[j, f, x] for j in range(m)]
            v = [states[k][f, DEEP + x] for k in range(steps)]
            terms = [b[j] * v[k] for j in range(m) for k in range(steps)]
            terms += [v[k] * v[l] for k, l in krylov_pairs]
            sums = [s + t for s, t in zip(sums, terms)]
        return sums

    new_sums = [zero] * first
    for f in range(fields):
        new_sums = new_products(f, new_sums)
    for i, s in enumerate(new_sums):
        rows[pl.ds(i, 1)] = jnp.sum(s, axis=0, keepdims=True)
    sums = jnp.sum(rows[...], axis=1, keepdims=True)
    at = lax.broadcasted_iota(jnp.int32, rows.shape, 0)
    spot = lax.broadcasted_iota(jnp.int32, rows.shape, 1)
    local = jnp.sum(jnp.where(at == spot, sums, 0.0), axis=0, keepdims=True)

    def summed(value, gathered, index, size, other, i):
        if size == 1:
            return value
        gathered[index] = value
        for d in range(1, size):
            pltpu.make_async_remote_copy(
                src_ref=gathered.at[index], dst_ref=gathered.at[index],
                send_sem=row_send.at[i], recv_sem=row_recv.at[i],
                device_id=other(d), device_id_type=MESH,
            ).start()
        others = gathered.at[pl.ds(0, size - 1)]
        everyone = pltpu.make_async_remote_copy(
            src_ref=others, dst_ref=others, send_sem=row_send.at[i], recv_sem=row_recv.at[i],
            device_id=other(1), device_id_type=MESH,
        )
        everyone.wait_recv()
        rows_sent.append(everyone)
        return jnp.sum(gathered[...], axis=0)

    rows_sent = []
    close = summed(local, near_rows, near_index, near_group, near_device, 0)
    sums_out[...] = summed(close, far_rows, far_index, far, far_device, 1)
    for copy in rows_sent:
        copy.wait_send()
    for copy in sends + plane_sends:
        copy.wait_send()
    for write in writes:
        write.wait()


def finish_kernel(
    ntot, chunks,
    sums, basis, krylov,
    proj_out, rfactor_out, new_out,
    result, out_sem,
):
    m, fields, planes = basis.shape[0], basis.shape[1], basis.shape[2]
    steps = krylov.shape[0]
    part = fields // chunks

    def piece(c):
        return pl.ds(c * part, part)

    shape = (8, basis.shape[4])
    row = sums[...] * (1.0 / ntot)

    def value(i):
        return jnp.broadcast_to(row[:, i : i + 1], shape)

    p = [[value(steps * j + k) for k in range(steps)] for j in range(m)]
    at = m * steps
    kk, bb = {}, {}
    for k in range(steps):
        for l in range(k, steps):
            kk[k, l] = value(at)
            at += 1
    for i in range(m):
        for j in range(i, m):
            bb[i, j] = bb[j, i] = value(at)
            at += 1
    q = [
        [2.0 * p[i][l] - total(bb[i, j] * p[j][l] for j in range(m)) for l in range(steps)]
        for i in range(m)
    ]
    low, inverse = {}, []
    for l in range(steps):
        for k in range(l, steps):
            g = kk[l, k] - total(p[i][l] * q[i][k] for i in range(m))
            for j in range(l):
                g = g - low[k, j] * low[l, j]
            if k == l:
                low[l, l] = jnp.sqrt(g)
                inverse.append(1.0 / low[l, l])
            else:
                low[k, l] = g * inverse[l]

    x = lax.broadcasted_iota(jnp.int32, shape, 0)
    y = lax.broadcasted_iota(jnp.int32, shape, 1)
    proj = jnp.zeros(shape, jnp.float32)
    for j in range(m):
        for k in range(steps):
            proj = jnp.where((x == j) & (y == k), p[j][k], proj)
    proj_out[...] = proj[:m, :steps]
    factor = jnp.zeros(shape, jnp.float32)
    for k, l in low:
        factor = jnp.where((x == l) & (y == k), low[k, l], factor)
    rfactor_out[...] = factor[:steps, :steps]

    writes = []
    for c in range(chunks):
        def one(i, carry, c=c):
            f = c * part + i
            for half in range(0, planes, 4):
                values = []
                for s in range(half, min(half + 4, planes)):
                    b = [basis[j, f, s] for j in range(m)]
                    done = []
                    for k in range(steps):
                        v = krylov[k, f, s] - total(p[j][k] * b[j] for j in range(m))
                        for l in range(k):
                            v = v - low[k, l] * done[l]
                        done.append(v * inverse[k])
                        values.append((k, s, done[k]))
                for k, s, value in values:
                    result[k, f, s] = value
            return carry

        for i in range(part):
            one(i, 0)
        write = pltpu.make_async_copy(
            result.at[:, piece(c)], new_out.at[:, piece(c)], out_sem.at[c]
        )
        write.start()
        writes.append(write)
    for write in writes:
        write.wait()


def on_device(streams, spans, basis, coeffs, mixing_matrix, base_speed, span_speed, polymer_gain):
    m, fields, planes, height, lanes = basis.shape
    n = streams * spans
    near, far = near_and_far(streams)
    f32 = jnp.float32
    deep = planes + 2 * DEEP
    count = m * STEPS + STEPS * (STEPS + 1) // 2 + m * (m + 1) // 2
    padded = -(-count // 8) * 8
    links = 2 + len(partners(spans))
    spans_beside = len(span_offsets(spans))
    corners = 2 + 2 * spans_beside
    tiles = -(-(fields + 3) * DEEP * WIDE // lanes)
    hbm = pl.BlockSpec(memory_space=pltpu.HBM)
    anywhere = pl.BlockSpec(memory_space=pl.ANY)
    vmem = pl.BlockSpec(memory_space=pltpu.VMEM)
    vector = (fields, planes, height, lanes)
    krylov, sums = pl.pallas_call(
        functools.partial(krylov_kernel, streams, spans),
        out_shape=(
            jax.ShapeDtypeStruct((STEPS,) + vector, f32),
            jax.ShapeDtypeStruct((1, lanes), f32),
        ),
        in_specs=[hbm] * 6,
        out_specs=(anywhere, vmem),
        scratch_shapes=[
            pltpu.VMEM((fields + 3, deep, height, lanes), f32),
            [pltpu.VMEM((fields, deep, height, lanes), f32)] * STEPS,
            pltpu.VMEM((m,) + vector, f32),
            pltpu.VMEM((fields + 3, height, lanes), f32),
            pltpu.VMEM((max(spans_beside, 1), fields + 3, height, lanes), f32),
            pltpu.VMEM((2, tiles, height, lanes), f32),
            pltpu.VMEM((corners, tiles, height, lanes), f32),
            [pltpu.VMEM((fields, 2, height, lanes), f32)] * STEPS,
            [pltpu.VMEM((fields, height, lanes), f32)] * STEPS,
            pltpu.VMEM((4, deep, height, lanes), f32),
            pltpu.VMEM((5, 2, height, lanes), f32),
            pltpu.VMEM((padded, lanes), f32),
            pltpu.VMEM((near * spans, 1, lanes), f32),
            pltpu.VMEM((far, 1, lanes), f32),
            pltpu.SMEM(coeffs.shape, f32),
            pltpu.SMEM(mixing_matrix.shape, f32),
            pltpu.SemaphoreType.DMA((10,)),
            pltpu.SemaphoreType.DMA((STEPS,)),
            pltpu.SemaphoreType.DMA((links,)),
            pltpu.SemaphoreType.DMA((links,)),
            pltpu.SemaphoreType.DMA((4,)),
            pltpu.SemaphoreType.DMA((4,)),
            pltpu.SemaphoreType.DMA((2,)),
            pltpu.SemaphoreType.DMA((2,)),
        ],
        compiler_params=pltpu.CompilerParams(
            collective_id=0, has_side_effects=True, vmem_limit_bytes=24 * 2**20
        ),
        name="krylov",
    )(*(
        pltpu.with_memory_space_constraint(x, pltpu.HBM)
        for x in (coeffs, mixing_matrix, basis, base_speed, span_speed, polymer_gain)
    ))
    chunks = 5 if fields % 5 == 0 else 1
    return pl.pallas_call(
        functools.partial(finish_kernel, float(m and basis[0].size * n), chunks),
        out_shape=(
            jax.ShapeDtypeStruct((m, STEPS), f32),
            jax.ShapeDtypeStruct((STEPS, STEPS), f32),
            jax.ShapeDtypeStruct((STEPS,) + vector, f32),
        ),
        in_specs=[vmem, vmem, vmem],
        out_specs=(vmem, vmem, hbm),
        scratch_shapes=[
            pltpu.VMEM((STEPS,) + vector, f32),
            pltpu.SemaphoreType.DMA((chunks,)),
        ],
        compiler_params=pltpu.CompilerParams(vmem_limit_bytes=24 * 2**20),
        name="finish",
    )(sums, basis, krylov)


def solution(mesh):
    placed = (
        P(None, None, "stream", None, "span"),
        P(),
        P(),
        P("stream", None, "span"),
        P("stream", None, "span"),
        P("stream", None, "span"),
    )
    return jax.shard_map(
        functools.partial(on_device, mesh.shape["stream"], mesh.shape["span"]),
        mesh=mesh,
        in_specs=placed,
        out_specs=(P(), P(), P(None, None, "stream", None, "span")),
        check_vma=False,
    )
```
